32 devices in a mesh: groups: 2 (over x), expert: 16 (over z, y, core).
Axes of the slice: x: 2, y: 2, z: 4, core: 2. Of those that a mesh axis runs over, the one named last changes fastest.
Arguments:
- tokens: bfloat16 [4096, 2048], P(('groups', 'expert')), parts along dimension 0, may hold values from -6 to 6
- expert_picks: int32 [4096, 6], P(('groups', 'expert')), parts along dimension 0, may hold values from 0 to 15, all different within a row; in each aligned block of 128 rows (0 to 127, 128 to 255, ...) at most 60 rows name the same one
- router: bfloat16 [2048, 16], replicated, may hold values from -0.125 to 0.125
- gate_weight: bfloat16 [16, 2048, 704], P('expert'), may hold values from -0.125 to 0.125
- up_weight: bfloat16 [16, 2048, 704], P('expert'), may hold values from -0.125 to 0.125
- down_weight: bfloat16 [16, 704, 2048], P('expert'), may hold values from -0.21875 to 0.21875
- image_rows: bfloat16 [32, 16, 8, 2048], P(('groups', 'expert')), parts along dimension 0, may hold values from -6 to 6
- image_counts: int32 [32, 16], P('groups'), parts along dimension 0, may hold values from 0 to 8
- span_owner: int32 [32], P('groups'), parts along dimension 0, may hold values from 0 to 15, each once
- text_rows: bfloat16 [4096, 2048], P(('groups', 'expert')), parts along dimension 0, may hold values from -6 to 6
Outputs:
- moe_out: bfloat16 [4096, 2048], P(('groups', 'expert')), parts along dimension 0
- next_span: bfloat16 [4096, 2048], P(('groups', 'expert')), parts along dimension 0
The draws below stay inside these ranges and needn't reach their ends.
There are 2 independent parts, one for each index of `groups`. The reference program is written for one: setup_inputs(seed, part) draws one part's arguments, and reference() takes and returns one part's arrays. A program takes and returns all parts, laid end to end along the dimension named above; an argument that names none is the same for every part. Nothing has to cross between parts.
Inputs may be any that keep to these rules, and one draw needn't show every extreme that they name: `expert_picks`: among one device's 128 rows no expert is picked more than 60 times; a token's 6 picks differ. `span_owner`: each device owns exactly one span.
All inputs are finite; a program needn't handle non-finite values.
Results may differ from the reference program's by a relative error of at most 0.0057.
Values may be sent and summed in bfloat16 or wider, within the bound.
No kernel may reach another device: no remote copies, remote signals or barrier semaphores. Data moves between devices by JAX's collectives and lax.ppermute only.
A program may use at most 128 MiB of HBM per device.

```python
import math
import jax
import jax.numpy as jnp
import numpy as np
from jax import lax

D = 2048
FF = 704
EXPERTS = 16
TOPK = 6
TOK_DEV = 128
TOKENS = 2048
CAP = 60
SLOT = 8
N_EXPERT = 16


def plant(entries, own_key, low, largest):
    place = [jax.random.randint(jax.random.fold_in(own_key, axis), (), 0, length) for axis, length in enumerate(entries.shape)]
    longest = entries.shape.index(max(entries.shape))
    neighbour = place[:longest] + [(place[longest] + 1) % entries.shape[longest]] + place[longest + 1:]
    return entries.at[tuple(place)].set(low).at[tuple(neighbour)].set(largest)


def steps_of(rng, extent, split, least, top_value):
    loudness = 1.0
    for dim, shards_of in split:
        draws = jax.random.uniform(jax.random.fold_in(jax.random.fold_in(rng, 6), dim), (shards_of,), jnp.float32, least / len(split), top_value / len(split))
        loudness = loudness * jnp.repeat(jnp.exp(draws), extent[dim] // shards_of).reshape((-1,) + (1,) * (len(extent) - 1 - dim))
    return loudness


def routed_block(own_key, own, number, rows, number_of, top, limit, lean):
    sequence = jax.random.permutation(own_key, number_of)
    crowded, common = portions_of(number_of, rows * top, limit, lean, True), portions_of(number_of, rows * top, limit, lean, False)
    places = jnp.arange(number_of)

    def named(lengths, turn):
        used = int((lengths > 0).sum())
        fixed = max(1, used // 4)
        passed = fixed + (places - fixed + turn * (used - fixed)) % max(1, number_of - fixed)
        return jnp.zeros((number_of,), jnp.int32).at[sequence[jnp.where(places < fixed, places, passed)]].set(jnp.asarray(lengths, jnp.int32))

    lengths = jnp.where(number % 4 == 0, named(crowded, number // 4), named(common, number - number // 4 - 1))
    mixed = jax.random.permutation(jax.random.fold_in(own, 3), number_of)
    donor, sink = mixed[0:number_of // 2 * 2:2], mixed[1:number_of // 2 * 2:2]
    slack = jnp.minimum(lengths[donor] - 1, limit - lengths[sink]) // 2
    slack = jnp.where((donor == sequence[0]) | (sink == sequence[0]) | (lengths[sink] == 0), 0, jnp.maximum(slack, 0))
    passed = jax.random.randint(jax.random.fold_in(own, 4), (number_of // 2,), 0, 1 << 20) % (slack + 1)
    lengths = lengths.at[donor].add(-passed).at[sink].add(passed)
    labels = jnp.searchsorted(jnp.cumsum(lengths), jnp.arange(rows * top), side="right").astype(jnp.int32)
    grid = labels.reshape(top, rows).T
    grid = grid[jax.random.permutation(jax.random.fold_in(own, 1), rows)]
    turn = jax.random.randint(jax.random.fold_in(own, 2), (rows, 1), 0, top)
    return jnp.take_along_axis(grid, (jnp.arange(top)[None, :] + turn) % top, axis=1)


def portions_of(amount, total, bound, lean, full):
    portions = [(1 << 20) // math.isqrt(grade ** lean) + 1 for grade in range(1, amount + 1)]
    largest = bound if full else min(bound, max(-(-total // amount), total * portions[0] // sum(portions)))
    least = 1 if total - largest >= amount - 1 else 0
    holding, rest = [largest] + [least] * (amount - 1), total - largest - least * (amount - 1)
    while rest > 0:
        candidates = [i for i in range(1, amount) if holding[i] < largest] or [i for i in range(1, amount) if holding[i] < bound]
        pool, budget = sum([portions[i] for i in candidates]), rest
        for i in candidates:
            addition = min(bound - holding[i], max(1, budget * portions[i] // pool), rest)
            holding[i] = holding[i] + addition
            rest = rest - addition
    return np.array(holding)


def bell_draw(key, dims, spread, most, shards=(), kind=jnp.bfloat16):
    loudness = steps_of(key, dims, shards, -0.22, 0.18) if shards else 1.0
    drawn = jax.random.normal(key, dims, jnp.float32) * spread * loudness
    return jnp.minimum(jnp.maximum(drawn, -most), most).astype(kind)


def setup_inputs(seed: int = 0, part: int = 0) -> dict:
    streams_of = jax.random.split(jax.random.key(seed), 11)
    part_splits = jax.random.split(jax.random.fold_in(streams_of[10], part), 11)
    tokens = bell_draw(part_splits[0], (TOKENS, D), 1.0, 6.0, ((0, 16),))
    expert_picks_keys = jax.random.split(jax.random.fold_in(part_splits[1], 1), TOKENS // TOK_DEV)
    expert_picks_turns = jax.random.permutation(jax.random.fold_in(part_splits[1], 3), TOKENS // TOK_DEV)
    expert_picks = jax.vmap(lambda own, number: routed_block(jax.random.fold_in(part_splits[1], 2), own, number, TOK_DEV, EXPERTS, TOPK, CAP, 2))(expert_picks_keys, expert_picks_turns).reshape((TOKENS, TOPK))
    router = bell_draw(streams_of[2], (D, EXPERTS), D ** -0.5, 0.125)
    gate_weight = bell_draw(streams_of[3], (EXPERTS, D, FF), D ** -0.5, 0.125, ((0, 16),))
    up_weight = bell_draw(streams_of[4], (EXPERTS, D, FF), D ** -0.5, 0.125, ((0, 16),))
    down_weight = bell_draw(streams_of[5], (EXPERTS, FF, D), FF ** -0.5, 0.21875, ((0, 16),))
    image_rows = bell_draw(part_splits[6], (N_EXPERT, N_EXPERT, SLOT, D), 1.0, 6.0, ((0, 16),))
    image_counts = plant(jax.random.randint(part_splits[7], (N_EXPERT, N_EXPERT), 0, SLOT + 1), jax.random.fold_in(part_splits[7], 1), 0, SLOT).astype(jnp.int32)
    span_owner = jax.random.permutation(part_splits[8], N_EXPERT).astype(jnp.int32)
    text_rows = bell_draw(part_splits[9], (TOKENS, D), 1.0, 6.0, ((0, 16),))
    return dict(tokens=tokens, expert_picks=expert_picks, router=router, gate_weight=gate_weight, up_weight=up_weight, down_weight=down_weight, image_rows=image_rows, image_counts=image_counts, span_owner=span_owner, text_rows=text_rows)


route_scale = 2.446


def place_images(arrived, column, text_block, slots):
    ends = jnp.cumsum(column).astype(jnp.int32)
    starts = (ends - column).astype(jnp.int32)
    total = ends[-1]
    position = jnp.arange(text_block.shape[0], dtype=jnp.int32)
    source = jnp.sum((position[:, None] >= ends[None, :]).astype(jnp.int32), axis=1).astype(jnp.int32)
    source = jnp.minimum(source, column.shape[0] - 1).astype(jnp.int32)
    offset = jnp.clip(position - starts[source], 0, slots - 1).astype(jnp.int32)
    picked = arrived[source * slots + offset]
    return jnp.where((position < total)[:, None], picked, text_block)


def expert_ffn(rows, gate_part, up_part, down_part):
    gate = jnp.dot(rows, gate_part, preferred_element_type=jnp.float32)
    upward = jnp.dot(rows, up_part, preferred_element_type=jnp.float32)
    hidden = (jax.nn.silu(gate) * upward).astype(jnp.bfloat16)
    return jnp.dot(hidden, down_part, preferred_element_type=jnp.float32).astype(jnp.bfloat16)


def reference(tokens, expert_picks, router, gate_weight, up_weight, down_weight, image_rows, image_counts, span_owner, text_rows):
    span_of = jnp.zeros((N_EXPERT,), jnp.int32).at[span_owner].set(jnp.arange(N_EXPERT, dtype=jnp.int32))
    text_blocks = text_rows.reshape(N_EXPERT, TOK_DEV, D)

    def assemble(owner_index):
        span = span_of[owner_index]
        column = image_counts[:, span]
        arrived = image_rows[:, span].reshape(N_EXPERT * SLOT, D)
        return place_images(arrived, column, text_blocks[owner_index], SLOT)

    next_span = jax.vmap(assemble)(jnp.arange(N_EXPERT, dtype=jnp.int32)).reshape(TOKENS, D)

    logits = jnp.dot(tokens, router, preferred_element_type=jnp.float32)
    score = jax.nn.sigmoid(logits)
    chosen = jnp.take_along_axis(score, expert_picks, axis=1)
    route = route_scale * chosen / jnp.sum(chosen, axis=1, keepdims=True)

    flat = expert_picks.reshape(-1)
    onehot = (flat[:, None] == jnp.arange(EXPERTS, dtype=jnp.int32)[None, :]).astype(jnp.int32)
    ranks = jnp.sum((jnp.cumsum(onehot, axis=0).astype(jnp.int32) - 1) * onehot, axis=1).astype(jnp.int32)
    per_expert = N_EXPERT * CAP
    target = (flat * per_expert + ranks).astype(jnp.int32)
    token_index = (jnp.arange(TOKENS * TOPK, dtype=jnp.int32) // TOPK).astype(jnp.int32)
    holder = jnp.zeros((EXPERTS * per_expert,), jnp.int32).at[target].set(token_index).reshape(EXPERTS, per_expert)

    def run_expert(packed):
        holder_row, gate_part, up_part, down_part = packed
        return expert_ffn(tokens[holder_row], gate_part, up_part, down_part)

    produced = lax.map(run_expert, (holder, gate_weight, up_weight, down_weight))
    gathered = produced.reshape(EXPERTS * per_expert, D)[target].reshape(TOKENS, TOPK, D)
    moe_out = jnp.sum(route[:, :, None] * gathered.astype(jnp.float32), axis=1).astype(jnp.bfloat16)
    return moe_out, next_span
```

```python
import functools

import jax
import jax.numpy as jnp
from jax import lax
from jax.experimental import pallas as pl
from jax.experimental.pallas import tpu as pltpu
from jax.sharding import PartitionSpec as P

route_scale = 2.446
NT = (((1,), (1,)), ((), ()))


def ring_of(chips):
    if chips <= 8:
        return list(range(0, chips, 2)) + list(range(chips - 1, 0, -2))
    return list(range(chips))


def pieces(total, step):
    return [(a, min(step, total - a)) for a in range(0, total, step)]


def ffn_kernel(count, sizes, columns, *refs):
    shards = refs[:count]
    route_ref, g0, u0, d0, g1, u1, d1 = refs[count : count + 7]
    outs = refs[count + 7 : count + 7 + len(columns)]
    x, hidden, total, wg, wu, wd, sems = refs[count + 7 + len(columns) :]
    rows = sum(sizes)
    ff = g0.shape[0]
    width = g0.shape[1]
    fs = pieces(ff, 256)
    copies = []
    for e, (g, u, d) in enumerate(((g0, u0, d0), (g1, u1, d1))):
        for i, (a, m) in enumerate(fs):
            copies.append(pltpu.make_async_copy(g.at[pl.ds(a, m)], wg.at[e, pl.ds(a, m)], sems.at[e, i, 0]))
            copies.append(pltpu.make_async_copy(u.at[pl.ds(a, m)], wu.at[e, pl.ds(a, m)], sems.at[e, i, 1]))
        copies.append(pltpu.make_async_copy(d, wd.at[e], sems.at[e, 0, 2]))
    for copy in copies:
        copy.start()
    at = 0
    for ref, m in zip(shards, sizes):
        x[pl.ds(at, m), :] = ref[...]
        at += m
    per = 2 * len(fs) + 1
    block = rows // len(columns)
    for e in range(2):
        for i, (a, m) in enumerate(fs):
            copies[e * per + 2 * i].wait()
            copies[e * per + 2 * i + 1].wait()
            gate = lax.dot_general(x[...], wg[e, pl.ds(a, m), :], NT, preferred_element_type=jnp.float32)
            upward = lax.dot_general(x[...], wu[e, pl.ds(a, m), :], NT, preferred_element_type=jnp.float32)
            hidden[:, pl.ds(a, m)] = (gate / (1.0 + jnp.exp(-gate)) * upward).astype(jnp.bfloat16)
        copies[e * per + per - 1].wait()

        @pl.loop(0, width // 256)
        def _(j):
            lanes = pl.ds(pl.multiple_of(j * 256, 256), 256)
            row = jnp.dot(hidden[...], wd[e, :, lanes], preferred_element_type=jnp.float32)
            row = row.astype(jnp.bfloat16).astype(jnp.float32)
            for k, c in enumerate(columns):
                part = row[k * block : (k + 1) * block] * route_ref[:, 2 * c + e : 2 * c + e + 1]
                if e == 0:
                    total[pl.ds(k * block, block), lanes] = part
                else:
                    outs[k][:, lanes] = (total[pl.ds(k * block, block), lanes] + part).astype(outs[k].dtype)


def ffn(shards, columns, route, weights, dtype):
    sizes = [s.shape[0] for s in shards]
    rows = sum(sizes)
    ff, width = weights[0].shape
    block = rows // len(columns)
    vmem = pl.BlockSpec(memory_space=pltpu.VMEM)
    hbm = pl.BlockSpec(memory_space=pl.ANY)
    return pl.pallas_call(
        functools.partial(ffn_kernel, len(shards), sizes, columns),
        out_shape=[jax.ShapeDtypeStruct((block, width), dtype) for _ in columns],
        in_specs=[vmem] * (len(shards) + 1) + [hbm] * 6,
        out_specs=[vmem] * len(columns),
        scratch_shapes=[
            pltpu.VMEM((rows, width), jnp.bfloat16),
            pltpu.VMEM((rows, ff), jnp.bfloat16),
            pltpu.VMEM((rows, width), jnp.float32),
            pltpu.VMEM((2, ff, width), jnp.bfloat16),
            pltpu.VMEM((2, ff, width), jnp.bfloat16),
            pltpu.VMEM((2, ff, width), jnp.bfloat16),
            pltpu.SemaphoreType.DMA((2, 3, 3)),
        ],
        compiler_params=pltpu.CompilerParams(vmem_limit_bytes=40 * 2**20),
        cost_estimate=pl.CostEstimate(
            flops=12 * rows * ff * width, bytes_accessed=12 * ff * width, transcendentals=2 * rows * ff
        ),
    )(*shards, route, *weights)


def place_kernel(slots, arrived_ref, counts_ref, owner_ref, me_ref, text_ref, out_ref):
    rows = text_ref.shape[0]
    devices = counts_ref.shape[0]
    held = arrived_ref.shape[0]
    mine = (owner_ref[...] == me_ref[0]).astype(jnp.int32)
    live = jnp.sum(counts_ref[...] * mine, axis=1, keepdims=True)
    total = jnp.sum(live)
    lane = lax.broadcasted_iota(jnp.int32, (devices, held), 1)
    holder = lane // slots
    which = lax.broadcasted_iota(jnp.int32, (devices, held), 0)
    own = jnp.sum(jnp.where(which == holder, live, 0), axis=0, keepdims=True)
    start = jnp.sum(jnp.where(which < holder, live, 0), axis=0, keepdims=True)
    offset = lane[:1] - holder[:1] * slots
    place = jnp.where(offset < own, start + offset, -1)
    row = lax.broadcasted_iota(jnp.int32, (rows, held), 0)
    pick = (row == place).astype(jnp.bfloat16)
    image = jnp.dot(pick, arrived_ref[...], preferred_element_type=jnp.float32).astype(jnp.bfloat16)
    position = lax.broadcasted_iota(jnp.int32, (rows, 1), 0)
    out_ref[...] = jnp.where(position < total, image, text_ref[...])


def place_images(arrived, counts, owner, me, text_block, slots):
    vmem = pl.BlockSpec(memory_space=pltpu.VMEM)
    return pl.pallas_call(
        functools.partial(place_kernel, slots),
        out_shape=jax.ShapeDtypeStruct(text_block.shape, text_block.dtype),
        in_specs=[vmem, vmem, vmem, pl.BlockSpec(memory_space=pltpu.SMEM), vmem],
        out_specs=vmem,
    )(arrived, counts, owner[None, :], me[None], text_block)


def local(
    tokens,
    expert_picks,
    router,
    gate_weight,
    up_weight,
    down_weight,
    image_rows,
    image_counts,
    span_owner,
    text_rows,
):
    devices = lax.axis_size("expert")
    me = lax.axis_index("expert")
    rows, width = tokens.shape
    half = rows // 2
    experts = gate_weight.shape[0] * devices
    slots = image_rows.shape[2]
    chips = devices // 2
    far = chips // 2
    ring = ring_of(chips)
    pos = {c: i for i, c in enumerate(ring)}

    def send(x, pairs):
        return lax.ppermute(x, "expert", pairs)

    def by_chip(target):
        return [(2 * c + k, 2 * target(c) + k) for c in range(chips) for k in range(2)]

    up = by_chip(lambda c: ring[(pos[c] + 1) % chips])
    down = by_chip(lambda c: ring[(pos[c] - 1) % chips])
    sibling = [(d, d ^ 1) for d in range(devices)]

    from_below, from_above = [tokens], [tokens]
    for s in range(1, far):
        from_below.append(send(from_below[-1], up))
        from_above.append(send(from_above[-1], down))
    last = [send(from_below[-1][:half], up), send(from_above[-1][half:], down)]

    own = [gate_weight[0].T, up_weight[0].T, down_weight[0]]
    weights = own + [send(w, sibling) for w in own]

    logits = lax.dot_general(router, tokens, (((0,), (1,)), ((), ())), preferred_element_type=jnp.float32)
    score = jax.nn.sigmoid(logits)
    expert = lax.broadcasted_iota(jnp.int32, (experts, rows), 0)
    picked = functools.reduce(
        jnp.logical_or, [expert == expert_picks[:, k][None, :] for k in range(expert_picks.shape[1])]
    )
    chosen = jnp.where(picked, score, 0.0)
    table = jnp.where(picked, route_scale * score / jnp.sum(chosen, axis=0, keepdims=True), 0.0)[None]
    bit = 1
    while bit < chips:
        table = jnp.concatenate([table, send(table, by_chip(lambda c: c ^ bit))], axis=0)
        bit *= 2
    chip = me // 2
    order = jnp.array(ring, jnp.int32)
    place = jnp.array([pos[c] for c in range(chips)], jnp.int32)[chip]
    source = order[(place + jnp.arange(chips, dtype=jnp.int32)) % chips] ^ chip
    wanted = (source[:, None] * experts + jnp.stack([me, me ^ 1])[None, :]).reshape(-1)
    route = table.reshape(chips * experts, rows)[wanted].T

    sums = {}
    for s in range(1, far):
        shards, columns = [from_above[s], from_below[s]], [s, chips - s]
        if s == 1:
            shards, columns = [tokens] + shards, [0] + columns
        for c, value in zip(columns, ffn(shards, columns, route, weights, jnp.float32)):
            sums[c] = value
    (farthest,) = ffn(last, [far], route, weights, jnp.bfloat16)

    def low(x):
        return x.astype(jnp.bfloat16)

    def wide(x):
        return x.astype(jnp.float32)

    going_down = send(farthest[:half], down)
    going_up = send(farthest[half:], up)
    going_down = low(sums[chips - far + 1] + jnp.pad(wide(going_down), ((0, rows - half), (0, 0))))
    going_up = low(sums[far - 1] + jnp.pad(wide(going_up), ((half, 0), (0, 0))))
    for s in range(far - 1, 0, -1):
        going_down = send(going_down, down)
        going_up = send(going_up, up)
        if s > 1:
            going_down = low(sums[chips - s + 1] + wide(going_down))
            going_up = low(sums[s - 1] + wide(going_up))
    moe_out = low(sums[0] + wide(going_down) + wide(going_up))

    number = jnp.arange(devices, dtype=jnp.int32)
    span_of = jnp.sum(jnp.where(span_owner[:, None] == number[None, :], number[:, None], 0), axis=0)
    image_send = image_rows[0][span_of]
    arrived = lax.all_to_all(image_send, "expert", split_axis=0, concat_axis=0, tiled=True)
    next_span = place_images(
        arrived.reshape(devices * slots, width), image_counts, span_owner, me, text_rows, slots
    )
    return (moe_out, next_span)


def solution(mesh):
    return jax.shard_map(
        local,
        mesh=mesh,
        in_specs=(
            P(("groups", "expert"), None),
            P(("groups", "expert"), None),
            P(),
            P("expert", None, None),
            P("expert", None, None),
            P("expert", None, None),
            P(("groups", "expert"), None, None, None),
            P("groups", None),
            P("groups"),
            P(("groups", "expert"), None),
        ),
        out_specs=(P(("groups", "expert"), None), P(("groups", "expert"), None)),
        check_vma=False,
    )
```

```python
import functools

import jax
import jax.numpy as jnp
from jax import lax
from jax.experimental import pallas as pl
from jax.experimental.pallas import tpu as pltpu
from jax.sharding import PartitionSpec as P

route_scale = 2.446
NT = (((1,), (1,)), ((), ()))


def ring_of(chips):
    if chips <= 8:
        return list(range(0, chips, 2)) + list(range(chips - 1, 0, -2))
    return list(range(chips))


def payload_kernel(picks_ref, router_ref, tokens_ref, out_ref):
    rows, width = tokens_ref.shape
    experts = router_ref.shape[0]
    spare = out_ref.shape[1] - width
    tokens = tokens_ref[...]
    out_ref[:, :width] = tokens
    logits = lax.dot_general(router_ref[...], tokens, NT, preferred_element_type=jnp.float32)
    score = 1.0 / (1.0 + jnp.exp(-logits))
    expert = lax.broadcasted_iota(jnp.int32, (experts, rows), 0)
    picked = expert == picks_ref[0:1, :]
    for k in range(1, picks_ref.shape[0]):
        picked = jnp.logical_or(picked, expert == picks_ref[k : k + 1, :])
    total = jnp.sum(jnp.where(picked, score, 0.0), axis=0, keepdims=True)
    route = jnp.where(picked, route_scale * score / total, 0.0)
    parts = []
    for _ in range(3):
        part = route.astype(jnp.bfloat16)
        parts.append(part.astype(jnp.float32))
        route = route - parts[-1]
    parts = jnp.concatenate(parts + [jnp.zeros((spare - 3 * experts, rows), jnp.float32)], axis=0)
    square = (rows, rows)
    eye = lax.broadcasted_iota(jnp.int32, square, 0) == lax.broadcasted_iota(jnp.int32, square, 1)
    turned = lax.dot_general(
        eye.astype(jnp.bfloat16), parts.astype(jnp.bfloat16), NT, preferred_element_type=jnp.float32
    )
    out_ref[:, width:] = turned.astype(jnp.bfloat16)


def payload_of(tokens, expert_picks, router):
    rows, width = tokens.shape
    spare = -(-3 * router.shape[1] // 128) * 128
    vmem = pl.BlockSpec(memory_space=pltpu.VMEM)
    return pl.pallas_call(
        payload_kernel,
        out_shape=jax.ShapeDtypeStruct((rows, width + spare), tokens.dtype),
        in_specs=[vmem] * 3,
        out_specs=vmem,
    )(expert_picks.T, router.T, tokens)


def ffn_kernel(count, sizes, experts, me_ref, *refs):
    shards = refs[:count]
    weights = refs[count : count + 6]
    outs = refs[count + 6 : -3]
    x, hidden, total = refs[-3:]
    rows = sum(sizes)
    width = x.shape[1]
    block = rows // len(outs)
    tails = []
    at = 0
    for ref, m in zip(shards, sizes):
        x[pl.ds(at, m), :] = ref[:, :width]
        tails.append(ref[:, width:].astype(jnp.float32))
        at += m
    tail = jnp.concatenate(tails, axis=0)
    lane = lax.broadcasted_iota(jnp.int32, tail.shape, 1)
    lane = jnp.where(lane < 3 * experts, lane % experts, -1)
    for e in range(2):
        wg, wu, wd = weights[3 * e : 3 * e + 3]
        wanted = me_ref[0] if e == 0 else me_ref[0] + 1 - 2 * (me_ref[0] % 2)
        route = jnp.sum(jnp.where(lane == wanted, tail, 0.0), axis=1, keepdims=True)
        gate = lax.dot_general(x[...], wg[...], NT, preferred_element_type=jnp.float32)
        upward = lax.dot_general(x[...], wu[...], NT, preferred_element_type=jnp.float32)
        hidden[...] = (gate / (1.0 + jnp.exp(-gate)) * upward).astype(jnp.bfloat16)
        for a in range(0, width, 512):
            lanes = pl.ds(a, 512)
            row = jnp.dot(hidden[...], wd[:, lanes], preferred_element_type=jnp.float32)
            row = row.astype(jnp.bfloat16).astype(jnp.float32) * route
            if e == 0:
                total[:, lanes] = row
            else:
                row = total[:, lanes] + row
                for k, out in enumerate(outs):
                    out[:, lanes] = row[k * block : (k + 1) * block].astype(out.dtype)


def ffn(shards, results, me, weights, experts, dtype):
    sizes = [s.shape[0] for s in shards]
    rows = sum(sizes)
    ff, width = weights[0].shape
    block = rows // results
    vmem = pl.BlockSpec(memory_space=pltpu.VMEM)
    return pl.pallas_call(
        functools.partial(ffn_kernel, len(shards), sizes, experts),
        out_shape=[jax.ShapeDtypeStruct((block, width), dtype)] * results,
        in_specs=[pl.BlockSpec(memory_space=pltpu.SMEM)] + [vmem] * (len(shards) + 6),
        out_specs=[vmem] * results,
        scratch_shapes=[
            pltpu.VMEM((rows, width), jnp.bfloat16),
            pltpu.VMEM((rows, ff), jnp.bfloat16),
            pltpu.VMEM((rows, width), jnp.float32),
        ],
        compiler_params=pltpu.CompilerParams(vmem_limit_bytes=30 * 2**20),
        cost_estimate=pl.CostEstimate(
            flops=12 * rows * ff * width, bytes_accessed=12 * ff * width, transcendentals=2 * rows * ff
        ),
    )(me[None], *shards, *weights)


def place_kernel(slots, arrived_ref, counts_ref, owner_ref, me_ref, text_ref, out_ref):
    rows = text_ref.shape[0]
    devices = counts_ref.shape[0]
    held = arrived_ref.shape[0]
    mine = (owner_ref[...] == me_ref[0]).astype(jnp.int32)
    live = jnp.sum(counts_ref[...] * mine, axis=1, keepdims=True)
    total = jnp.sum(live)
    lane = lax.broadcasted_iota(jnp.int32, (devices, held), 1)
    holder = lane // slots
    which = lax.broadcasted_iota(jnp.int32, (devices, held), 0)
    own = jnp.sum(jnp.where(which == holder, live, 0), axis=0, keepdims=True)
    start = jnp.sum(jnp.where(which < holder, live, 0), axis=0, keepdims=True)
    offset = lane[:1] - holder[:1] * slots
    place = jnp.where(offset < own, start + offset, -1)
    row = lax.broadcasted_iota(jnp.int32, (rows, held), 0)
    pick = (row == place).astype(jnp.bfloat16)
    image = jnp.dot(pick, arrived_ref[...], preferred_element_type=jnp.float32).astype(jnp.bfloat16)
    position = lax.broadcasted_iota(jnp.int32, (rows, 1), 0)
    out_ref[...] = jnp.where(position < total, image, text_ref[...])


def place_images(arrived, counts, owner, me, text_block, slots):
    vmem = pl.BlockSpec(memory_space=pltpu.VMEM)
    return pl.pallas_call(
        functools.partial(place_kernel, slots),
        out_shape=jax.ShapeDtypeStruct(text_block.shape, text_block.dtype),
        in_specs=[vmem, vmem, vmem, pl.BlockSpec(memory_space=pltpu.SMEM), vmem],
        out_specs=vmem,
    )(arrived, counts, owner[None, :], me[None], text_block)


def local(
    tokens,
    expert_picks,
    router,
    gate_weight,
    up_weight,
    down_weight,
    image_rows,
    image_counts,
    span_owner,
    text_rows,
):
    devices = lax.axis_size("expert")
    me = lax.axis_index("expert")
    rows, width = tokens.shape
    half = rows // 2
    experts = gate_weight.shape[0] * devices
    slots = image_rows.shape[2]
    chips = devices // 2
    far = chips // 2
    ring = ring_of(chips)
    pos = {c: i for i, c in enumerate(ring)}

    def send(x, pairs):
        return lax.ppermute(x, "expert", pairs)

    def by_chip(target):
        return [(2 * c + k, 2 * target(c) + k) for c in range(chips) for k in range(2)]

    up = by_chip(lambda c: ring[(pos[c] + 1) % chips])
    down = by_chip(lambda c: ring[(pos[c] - 1) % chips])
    sibling = [(d, d ^ 1) for d in range(devices)]

    own = [gate_weight[0].T, up_weight[0].T, down_weight[0]]
    weights = own + [send(w, sibling) for w in own]
    weights = [pltpu.with_memory_space_constraint(w, pltpu.VMEM) for w in weights]

    mine = payload_of(tokens, expert_picks, router)
    from_below, from_above = [mine], [mine]
    for s in range(1, far):
        from_below.append(send(from_below[-1], up))
        from_above.append(send(from_above[-1], down))
    last = [send(from_below[-1][:half], up), send(from_above[-1][half:], down)]

    sums = {}
    for s in range(1, far):
        shards, columns = [from_above[s], from_below[s]], [s, chips - s]
        if s == 1:
            shards, columns = [mine] + shards, [0] + columns
        for c, value in zip(columns, ffn(shards, len(columns), me, weights, experts, jnp.float32)):
            sums[c] = value
    (farthest,) = ffn(last, 1, me, weights, experts, jnp.bfloat16)

    def low(x):
        return x.astype(jnp.bfloat16)

    def wide(x):
        return x.astype(jnp.float32)

    going_down = send(farthest[:half], down)
    going_up = send(farthest[half:], up)
    going_down = low(sums[chips - far + 1] + jnp.pad(wide(going_down), ((0, rows - half), (0, 0))))
    going_up = low(sums[far - 1] + jnp.pad(wide(going_up), ((half, 0), (0, 0))))
    for s in range(far - 1, 0, -1):
        going_down = send(going_down, down)
        going_up = send(going_up, up)
        if s > 1:
            going_down = low(sums[chips - s + 1] + wide(going_down))
            going_up = low(sums[s - 1] + wide(going_up))
    moe_out = low(sums[0] + wide(going_down) + wide(going_up))

    number = jnp.arange(devices, dtype=jnp.int32)
    span_of = jnp.sum(jnp.where(span_owner[:, None] == number[None, :], number[:, None], 0), axis=0)
    image_send, _ = lax.optimization_barrier((image_rows[0][span_of], from_below[-1]))
    arrived = lax.all_to_all(image_send, "expert", split_axis=0, concat_axis=0, tiled=True)
    next_span = place_images(
        arrived.reshape(devices * slots, width), image_counts, span_owner, me, text_rows, slots
    )
    return (moe_out, next_span)


def solution(mesh):
    return jax.shard_map(
        local,
        mesh=mesh,
        in_specs=(
            P(("groups", "expert"), None),
            P(("groups", "expert"), None),
            P(),
            P("expert", None, None),
            P("expert", None, None),
            P("expert", None, None),
            P(("groups", "expert"), None, None, None),
            P("groups", None),
            P("groups"),
            P(("groups", "expert"), None),
        ),
        out_specs=(P(("groups", "expert"), None), P(("groups", "expert"), None)),
        check_vma=False,
    )
```

```python
import functools
import math

import jax
import jax.numpy as jnp
from jax import lax
from jax.experimental import pallas as pl
from jax.experimental.pallas import tpu as pltpu
from jax.sharding import PartitionSpec as P

route_scale = 2.446
NT = (((1,), (1,)), ((), ()))


def ring_of(chips):
    if chips <= 8:
        return list(range(0, chips, 2)) + list(range(chips - 1, 0, -2))
    return list(range(chips))


def route_kernel(slots, picks_ref, router_hbm, tokens_hbm, out_ref, router_ref, tokens_ref, sems):
    rows = tokens_ref.shape[0]
    experts = router_ref.shape[0]
    take_tokens = pltpu.make_async_copy(tokens_hbm, tokens_ref, sems.at[0])
    take_router = pltpu.make_async_copy(router_hbm, router_ref, sems.at[1])
    take_tokens.start()
    take_router.start()
    take_tokens.wait()
    take_router.wait()
    logits = lax.dot_general(router_ref[...], tokens_ref[...], NT, preferred_element_type=jnp.float32)
    score = 1.0 / (1.0 + jnp.exp(-logits))
    expert = lax.broadcasted_iota(jnp.int32, (experts, rows), 0)
    picked = expert == picks_ref[0:1, :]
    for k in range(1, picks_ref.shape[0]):
        picked = jnp.logical_or(picked, expert == picks_ref[k : k + 1, :])
    total = jnp.sum(jnp.where(picked, score, 0.0), axis=0, keepdims=True)
    route = jnp.where(picked, route_scale * score / total, 0.0)
    parts = []
    for _ in range(3):
        part = route.astype(jnp.bfloat16)
        parts.append(part.astype(jnp.float32))
        route = route - parts[-1]
    parts = jnp.concatenate(parts, axis=0).astype(jnp.bfloat16)
    shape = (out_ref.shape[0], 3 * experts)
    target = lax.broadcasted_iota(jnp.int32, shape, 0)
    source = lax.broadcasted_iota(jnp.int32, shape, 1)
    for block in range(out_ref.shape[1] // rows):
        line = block * slots + target % slots
        wanted = (line % 3) * experts + ((target // slots) ^ (line // 3))
        pick = jnp.logical_and(line < 6, source == wanted).astype(jnp.bfloat16)
        out_ref[:, block * rows : (block + 1) * rows] = jnp.dot(
            pick, parts, preferred_element_type=jnp.float32
        ).astype(jnp.bfloat16)


def in_hbm(x):
    return pltpu.with_memory_space_constraint(x, pltpu.HBM)


def route_of(tokens, expert_picks, router, slots):
    rows, width = tokens.shape
    experts = router.shape[1]
    vmem = pl.BlockSpec(memory_space=pltpu.VMEM)
    hbm = pl.BlockSpec(memory_space=pl.ANY)
    return pl.pallas_call(
        functools.partial(route_kernel, slots),
        out_shape=jax.ShapeDtypeStruct((experts * slots, -(-6 // slots) * rows), jnp.bfloat16),
        in_specs=[vmem, hbm, hbm],
        out_specs=vmem,
        scratch_shapes=[
            pltpu.VMEM((experts, width), router.dtype),
            pltpu.VMEM((rows, width), tokens.dtype),
            pltpu.SemaphoreType.DMA((2,)),
        ],
        compiler_params=pltpu.CompilerParams(vmem_limit_bytes=8 * 2**20),
    )(expert_picks.T, in_hbm(router.T), in_hbm(tokens))


def lines_kernel(width, slots, arrived_hbm, out_ref, taken_ref, sem):
    copy = pltpu.make_async_copy(arrived_hbm.at[:, pl.ds(width, taken_ref.shape[1])], taken_ref, sem)
    copy.start()
    copy.wait()
    lines, rows = out_ref.shape
    shape = (lines, taken_ref.shape[0])
    target = lax.broadcasted_iota(jnp.int32, shape, 0)
    source = lax.broadcasted_iota(jnp.int32, shape, 1)
    total = jnp.zeros(out_ref.shape, jnp.float32)
    for block in range(taken_ref.shape[1] // rows):
        line = target % 8 - block * slots
        wanted = jnp.where(jnp.logical_and(line >= 0, line < slots), target // 8 * slots + line, -1)
        pick = (source == wanted).astype(jnp.bfloat16)
        total = total + jnp.dot(
            pick, taken_ref[:, block * rows : (block + 1) * rows], preferred_element_type=jnp.float32
        )
    out_ref[...] = total


def lines_of(arrived, width, slots, rows):
    devices = arrived.shape[0] // slots
    return pl.pallas_call(
        functools.partial(lines_kernel, width, slots),
        out_shape=jax.ShapeDtypeStruct((8 * devices, rows), jnp.float32),
        in_specs=[pl.BlockSpec(memory_space=pl.ANY)],
        out_specs=pl.BlockSpec(memory_space=pltpu.VMEM),
        scratch_shapes=[
            pltpu.VMEM((arrived.shape[0], arrived.shape[1] - width), arrived.dtype),
            pltpu.SemaphoreType.DMA,
        ],
        compiler_params=pltpu.CompilerParams(vmem_limit_bytes=4 * 2**20),
    )(arrived)


def spans_kernel(span_of_ref, rows_hbm, out_ref, sems):
    copies = [
        pltpu.make_async_copy(rows_hbm.at[span_of_ref[d]], out_ref.at[d], sems.at[d]) for d in range(rows_hbm.shape[0])
    ]
    for copy in copies:
        copy.start()
    for copy in copies:
        copy.wait()


def by_owner(image_rows, span_of):
    return pl.pallas_call(
        spans_kernel,
        out_shape=jax.ShapeDtypeStruct(image_rows.shape, image_rows.dtype),
        in_specs=[pl.BlockSpec(memory_space=pltpu.SMEM), pl.BlockSpec(memory_space=pl.ANY)],
        out_specs=pl.BlockSpec(memory_space=pltpu.VMEM),
        scratch_shapes=[pltpu.SemaphoreType.DMA((image_rows.shape[0],))],
        compiler_params=pltpu.CompilerParams(vmem_limit_bytes=4 * 2**20),
    )(span_of, in_hbm(image_rows))


def ffn_kernel(count, results, sizes, offsets, chips, holds, me_ref, order_ref, *refs):
    shards = refs[:count]
    table = refs[count]
    weights = refs[count + 1 : count + 7]
    outs = refs[count + 7 : count + 7 + results]
    kept = refs[count + 7 + results : count + 7 + results + holds]
    x, hidden, total = refs[count + 7 + results + holds :][:3]
    copies = []
    if holds:
        sems = refs[-1]
        for i in range(6):
            copies.append(pltpu.make_async_copy(weights[i], kept[i], sems.at[i]))
            copies[i].start()
        weights = kept
    rows = sum(sizes)
    width = x.shape[1]
    block = rows // results
    at = 0
    for ref, m in zip(shards, sizes):
        x[pl.ds(at, m), :] = ref[...]
        at += m
    me = me_ref[0]
    tokens = rows // len(offsets)
    square = (tokens, tokens)
    eye = lax.broadcasted_iota(jnp.int32, square, 0) == lax.broadcasted_iota(jnp.int32, square, 1)
    routes = [[], []]
    for offset in offsets:
        source = 2 * order_ref[(me // 2) * chips + offset] + me % 2
        lines = table[pl.ds(pl.multiple_of(source * 8, 8), 8), :]
        for e in range(2):
            line = lines[3 * e : 3 * e + 1] + lines[3 * e + 1 : 3 * e + 2] + lines[3 * e + 2 : 3 * e + 3]
            routes[e].append(jnp.sum(jnp.where(eye, line, 0.0), axis=1, keepdims=True))
    for e in range(2):
        wg, wu, wd = weights[3 * e : 3 * e + 3]
        route = jnp.concatenate(routes[e], axis=0)
        if holds:
            copies[3 * e].wait()
            copies[3 * e + 1].wait()
        gate = lax.dot_general(x[...], wg[...], NT, preferred_element_type=jnp.float32)
        upward = lax.dot_general(x[...], wu[...], NT, preferred_element_type=jnp.float32)
        hidden[...] = (gate / (1.0 + jnp.exp(-gate)) * upward).astype(jnp.bfloat16)
        if holds:
            copies[3 * e + 2].wait()
        for a in range(0, width, 512):
            lanes = pl.ds(a, 512)
            row = jnp.dot(hidden[...], wd[:, lanes], preferred_element_type=jnp.float32)
            row = row.astype(jnp.bfloat16).astype(jnp.float32) * route
            if e == 0:
                total[:, lanes] = row
            else:
                row = total[:, lanes] + row
                for k, out in enumerate(outs):
                    out[:, lanes] = row[k * block : (k + 1) * block].astype(out.dtype)


def ffn(shards, offsets, results, me, order, table, weights, holds):
    sizes = [s.shape[0] for s in shards]
    rows = sum(sizes)
    ff, width = weights[0].shape
    block = rows // results
    vmem = pl.BlockSpec(memory_space=pltpu.VMEM)
    smem = pl.BlockSpec(memory_space=pltpu.SMEM)
    hbm = pl.BlockSpec(memory_space=pl.ANY)
    chips = math.isqrt(order.shape[0])
    kept = 6 if holds else 0
    if holds:
        weights = [in_hbm(w) for w in weights]
    return pl.pallas_call(
        functools.partial(ffn_kernel, len(shards), results, sizes, offsets, chips, kept),
        out_shape=[jax.ShapeDtypeStruct((block, width), jnp.float32)] * results
        + [pltpu.VMEM(w.shape, w.dtype) for w in weights[:kept]],
        in_specs=[smem] * 2 + [vmem] * (len(shards) + 1) + [hbm if holds else vmem] * 6,
        out_specs=[vmem] * (results + kept),
        scratch_shapes=[
            pltpu.VMEM((rows, width), jnp.bfloat16),
            pltpu.VMEM((rows, ff), jnp.bfloat16),
            pltpu.VMEM((rows, width), jnp.float32),
        ]
        + [pltpu.SemaphoreType.DMA((6,))] * holds,
        compiler_params=pltpu.CompilerParams(vmem_limit_bytes=10 * 2**20),
        cost_estimate=pl.CostEstimate(
            flops=12 * rows * ff * width, bytes_accessed=12 * ff * width, transcendentals=2 * rows * ff
        ),
    )(me[None], order, *shards, table, *weights)


def place_kernel(slots, arrived_ref, counts_ref, owner_ref, me_ref, text_ref, out_ref):
    rows = text_ref.shape[0]
    devices = counts_ref.shape[0]
    held = arrived_ref.shape[0]
    mine = (owner_ref[...] == me_ref[0]).astype(jnp.int32)
    live = jnp.sum(counts_ref[...] * mine, axis=1, keepdims=True)
    total = jnp.sum(live)
    lane = lax.broadcasted_iota(jnp.int32, (devices, held), 1)
    holder = lane // slots
    which = lax.broadcasted_iota(jnp.int32, (devices, held), 0)
    own = jnp.sum(jnp.where(which == holder, live, 0), axis=0, keepdims=True)
    start = jnp.sum(jnp.where(which < holder, live, 0), axis=0, keepdims=True)
    offset = lane[:1] - holder[:1] * slots
    place = jnp.where(offset < own, start + offset, -1)
    row = lax.broadcasted_iota(jnp.int32, (rows, held), 0)
    pick = (row == place).astype(jnp.bfloat16)
    image = jnp.dot(pick, arrived_ref[:, : text_ref.shape[1]], preferred_element_type=jnp.float32).astype(jnp.bfloat16)
    position = lax.broadcasted_iota(jnp.int32, (rows, 1), 0)
    out_ref[...] = jnp.where(position < total, image, text_ref[...])


def place_images(arrived, counts, owner, me, text_block, slots):
    vmem = pl.BlockSpec(memory_space=pltpu.VMEM)
    return pl.pallas_call(
        functools.partial(place_kernel, slots),
        out_shape=jax.ShapeDtypeStruct(text_block.shape, text_block.dtype),
        in_specs=[vmem, vmem, vmem, pl.BlockSpec(memory_space=pltpu.SMEM), vmem],
        out_specs=vmem,
        compiler_params=pltpu.CompilerParams(vmem_limit_bytes=8 * 2**20),
    )(arrived, counts, owner[None, :], me[None], text_block)


def cut_kernel(below_ref, above_ref, first_ref, second_ref, sems):
    half = first_ref.shape[0]
    copies = [
        pltpu.make_async_copy(below_ref.at[pl.ds(0, half)], first_ref, sems.at[0]),
        pltpu.make_async_copy(above_ref.at[pl.ds(half, half)], second_ref, sems.at[1]),
    ]
    for copy in copies:
        copy.start()
    for copy in copies:
        copy.wait()


def cut(below, above):
    rows, width = below.shape
    vmem = pl.BlockSpec(memory_space=pltpu.VMEM)
    return pl.pallas_call(
        cut_kernel,
        out_shape=[jax.ShapeDtypeStruct((rows // 2, width), below.dtype)] * 2,
        in_specs=[pl.BlockSpec(memory_space=pl.ANY)] * 2,
        out_specs=[vmem] * 2,
        scratch_shapes=[pltpu.SemaphoreType.DMA((2,))],
        compiler_params=pltpu.CompilerParams(vmem_limit_bytes=2 * 2**20),
    )(below, above)


def merge_kernel(above_ref, below_ref, up_first, up_second, down_first, down_second, up_ref, down_ref):
    half = up_first.shape[0]
    for out, total, first, second in (
        (up_ref, above_ref, up_first, up_second),
        (down_ref, below_ref, down_first, down_second),
    ):
        for i, came in enumerate((first, second)):
            part = pl.ds(i * half, half)
            out[part, :] = (total[part, :] + came[...].astype(jnp.float32)).astype(out.dtype)


def merge(above, below, *came):
    vmem = pl.BlockSpec(memory_space=pltpu.VMEM)
    return pl.pallas_call(
        merge_kernel,
        out_shape=[jax.ShapeDtypeStruct(above.shape, jnp.bfloat16)] * 2,
        in_specs=[vmem] * 6,
        out_specs=[vmem] * 2,
        compiler_params=pltpu.CompilerParams(vmem_limit_bytes=8 * 2**20),
    )(above, below, *came)


def tie(*arrays):
    return lax.optimization_barrier(arrays)


def local(
    tokens,
    expert_picks,
    router,
    gate_weight,
    up_weight,
    down_weight,
    image_rows,
    image_counts,
    span_owner,
    text_rows,
):
    devices = lax.axis_size("expert")
    me = lax.axis_index("expert")
    width = tokens.shape[1]
    experts = gate_weight.shape[0] * devices
    slots = image_rows.shape[2]
    chips = devices // 2
    far = chips // 2
    ring = ring_of(chips)
    pos = {c: i for i, c in enumerate(ring)}

    def send(x, pairs):
        return lax.ppermute(x, "expert", pairs)

    up = [(2 * c + k, 2 * ring[(pos[c] + 1) % chips] + k) for c in range(chips) for k in range(2)]
    down = [(target, source) for source, target in up]
    sibling = [(d, d ^ 1) for d in range(devices)]

    own = [gate_weight[0].T, up_weight[0].T, down_weight[0]]
    others = [send(w, sibling) for w in own]

    order = jnp.array([ring[(pos[c] + offset) % chips] for c in range(chips) for offset in range(chips)], jnp.int32)

    def run(shards, offsets, results=None, holds=False):
        return ffn(shards, offsets, results or len(shards), me, order, table, weights, holds)

    def run_both(s):
        return run([below[s], above[s]], [chips - s, s])

    number = jnp.arange(devices, dtype=jnp.int32)
    span_of = jnp.sum(jnp.where(span_owner[:, None] == number[None, :], number[:, None], 0), axis=0)
    span_of, expert_picks, swapped = tie(span_of, expert_picks, others[0])
    lines = route_of(tokens, expert_picks, router, slots)
    image_send = jnp.concatenate([by_owner(image_rows[0], span_of), lines.reshape(devices, slots, -1)], axis=2)
    arrived = lax.all_to_all(image_send, "expert", split_axis=0, concat_axis=0, tiled=True)
    arrived = arrived.reshape(devices * slots, -1)

    below, above = [tokens], [tokens]
    from_below, from_above = {}, {}
    for s in range(1, far):
        below.append(send(below[-1], up))
        above.append(send(above[-1], down))
        below[s], above[s] = tie(below[s], above[s])
    table = lines_of(arrived, width, slots, tokens.shape[0])
    weights = own + others

    first, second = cut(below[-1], above[-1])
    first, second = send(first, up), send(second, down)
    *done, w0, w1, w2, w3, w4, w5 = run([below[-1], above[-1]], [chips - far + 1, far - 1], 4, True)
    weights = [w0, w1, w2, w3, w4, w5]
    first, second, *done = tie(first, second, *done)

    def low(x):
        return x.astype(jnp.bfloat16)

    def add(mine, came):
        return low(mine + came.astype(jnp.float32))

    below_first, below_second, above_first, above_second = done
    short_up, short_down = send(low(above_first), up), send(low(below_second), down)
    far_first, far_second, result_first, result_second = run([first, second, tokens], [far, 0], 4)
    short_up, short_down, far_first, far_second = tie(short_up, short_down, far_first, far_second)
    long_up, long_down = send(low(far_second), up), send(low(far_first), down)
    from_below[far - 2], from_above[far - 2] = run_both(far - 2)
    long_up, long_down, from_below[far - 2], from_above[far - 2] = tie(
        long_up, long_down, from_below[far - 2], from_above[far - 2]
    )
    long_up, long_down = send(add(above_second, long_up), up), send(add(below_first, long_down), down)
    from_below[1], from_above[1] = run_both(1)
    long_up, long_down, from_below[1], from_above[1] = tie(long_up, long_down, from_below[1], from_above[1])
    going_up, going_down = merge(
        from_above[far - 2], from_below[far - 2], short_up, long_up, long_down, short_down
    )
    for s in range(2, far - 2):
        if s not in from_below:
            from_below[s], from_above[s] = run_both(s)
    for s in range(far - 2, 0, -1):
        going_up, going_down = tie(send(going_up, up), send(going_down, down))
        if s > 1:
            going_up, going_down = add(from_above[s - 1], going_up), add(from_below[s - 1], going_down)
    result = jnp.concatenate([result_first, result_second], axis=0)
    moe_out = low(result + going_up.astype(jnp.float32) + going_down.astype(jnp.float32))

    next_span = place_images(
        arrived, image_counts, span_owner, me, text_rows, slots
    )
    return (moe_out, next_span)


def solution(mesh):
    return jax.shard_map(
        local,
        mesh=mesh,
        in_specs=(
            P(("groups", "expert"), None),
            P(("groups", "expert"), None),
            P(),
            P("expert", None, None),
            P("expert", None, None),
            P("expert", None, None),
            P(("groups", "expert"), None, None, None),
            P("groups", None),
            P("groups"),
            P(("groups", "expert"), None),
        ),
        out_specs=(P(("groups", "expert"), None), P(("groups", "expert"), None)),
        check_vma=False,
    )
```

```python
import functools
import math

import jax
import jax.numpy as jnp
from jax import lax
from jax.experimental import pallas as pl
from jax.experimental.pallas import tpu as pltpu
from jax.sharding import PartitionSpec as P

route_scale = 2.446
NT = (((1,), (1,)), ((), ()))


def ring_of(chips):
    if chips <= 8:
        return list(range(0, chips, 2)) + list(range(chips - 1, 0, -2))
    return list(range(chips))


def route_kernel(picks_ref, router_hbm, tokens_hbm, out_ref, router_ref, tokens_ref, sems):
    experts = router_ref.shape[0]
    rows = tokens_ref.shape[0]
    take_tokens = pltpu.make_async_copy(tokens_hbm, tokens_ref, sems.at[0])
    take_router = pltpu.make_async_copy(router_hbm, router_ref, sems.at[1])
    take_tokens.start()
    take_router.start()
    take_tokens.wait()
    take_router.wait()
    logits = lax.dot_general(router_ref[...], tokens_ref[...], NT, preferred_element_type=jnp.float32)
    score = 1.0 / (1.0 + jnp.exp(-logits))
    expert = lax.broadcasted_iota(jnp.int32, (experts, rows), 0)
    picked = expert == picks_ref[0:1, :]
    for k in range(1, picks_ref.shape[0]):
        picked = jnp.logical_or(picked, expert == picks_ref[k : k + 1, :])
    total = jnp.sum(jnp.where(picked, score, 0.0), axis=0, keepdims=True)
    rest = jnp.where(picked, route_scale * score / total, 0.0)
    target = lax.broadcasted_iota(jnp.int32, (out_ref.shape[0], experts), 0)
    source = lax.broadcasted_iota(jnp.int32, (out_ref.shape[0], experts), 1)
    pick = jnp.logical_and(target % 8 < 2, source == ((target // 8) ^ (target % 8))).astype(jnp.bfloat16)
    lines = jnp.zeros(out_ref.shape, jnp.float32)
    for _ in range(3):
        part = rest.astype(jnp.bfloat16)
        rest = rest - part.astype(jnp.float32)
        lines = lines + jnp.dot(pick, part, preferred_element_type=jnp.float32)
    out_ref[...] = lines


def in_hbm(x):
    return pltpu.with_memory_space_constraint(x, pltpu.HBM)


def route_of(tokens, expert_picks, router):
    rows, width = tokens.shape
    experts = router.shape[1]
    vmem = pl.BlockSpec(memory_space=pltpu.VMEM)
    hbm = pl.BlockSpec(memory_space=pl.ANY)
    return pl.pallas_call(
        route_kernel,
        out_shape=jax.ShapeDtypeStruct((8 * experts, rows), jnp.float32),
        in_specs=[vmem, hbm, hbm],
        out_specs=vmem,
        scratch_shapes=[
            pltpu.VMEM((experts, width), router.dtype),
            pltpu.VMEM((rows, width), tokens.dtype),
            pltpu.SemaphoreType.DMA((2,)),
        ],
        compiler_params=pltpu.CompilerParams(vmem_limit_bytes=8 * 2**20),
    )(expert_picks.T, in_hbm(router.T), in_hbm(tokens))


def spans_kernel(span_of_ref, rows_hbm, out_ref, sems):
    copies = [
        pltpu.make_async_copy(rows_hbm.at[span_of_ref[d]], out_ref.at[d], sems.at[d]) for d in range(rows_hbm.shape[0])
    ]
    for copy in copies:
        copy.start()
    for copy in copies:
        copy.wait()


def by_owner(image_rows, span_of):
    return pl.pallas_call(
        spans_kernel,
        out_shape=jax.ShapeDtypeStruct(image_rows.shape, image_rows.dtype),
        in_specs=[pl.BlockSpec(memory_space=pltpu.SMEM), pl.BlockSpec(memory_space=pl.ANY)],
        out_specs=pl.BlockSpec(memory_space=pltpu.VMEM),
        scratch_shapes=[pltpu.SemaphoreType.DMA((image_rows.shape[0],))],
        compiler_params=pltpu.CompilerParams(vmem_limit_bytes=4 * 2**20),
    )(span_of, in_hbm(image_rows))


def ffn_kernel(count, results, sizes, offsets, chips, holds, me_ref, order_ref, *refs):
    shards = refs[:count]
    table = refs[count]
    weights = refs[count + 1 : count + 7]
    outs = refs[count + 7 : count + 7 + results]
    kept = refs[count + 7 + results : count + 7 + results + holds]
    x, hidden, total = refs[count + 7 + results + holds :][:3]
    copies = []
    if holds:
        sems = refs[-1]
        for i in range(6):
            copies.append(pltpu.make_async_copy(weights[i], kept[i], sems.at[i]))
            copies[i].start()
        weights = kept
    rows = sum(sizes)
    width = x.shape[1]
    block = rows // results
    at = 0
    for ref, m in zip(shards, sizes):
        x[pl.ds(at, m), :] = ref[...]
        at += m
    me = me_ref[0]
    tokens = rows // len(offsets)
    square = (tokens, tokens)
    eye = lax.broadcasted_iota(jnp.int32, square, 0) == lax.broadcasted_iota(jnp.int32, square, 1)
    routes = [[], []]
    for offset in offsets:
        source = 2 * order_ref[(me // 2) * chips + offset] + me % 2
        lines = table[pl.ds(pl.multiple_of(source * 8, 8), 8), :]
        for e in range(2):
            routes[e].append(jnp.sum(jnp.where(eye, lines[e : e + 1], 0.0), axis=1, keepdims=True))
    for e in range(2):
        wg, wu, wd = weights[3 * e : 3 * e + 3]
        route = jnp.concatenate(routes[e], axis=0)
        if holds:
            copies[3 * e].wait()
        gate = lax.dot_general(x[...], wg[...], NT, preferred_element_type=jnp.float32)
        if holds:
            copies[3 * e + 1].wait()
        upward = lax.dot_general(x[...], wu[...], NT, preferred_element_type=jnp.float32)
        hidden[...] = (gate / (1.0 + jnp.exp(-gate)) * upward).astype(jnp.bfloat16)
        if holds:
            copies[3 * e + 2].wait()
        for a in range(0, width, 512):
            lanes = pl.ds(a, 512)
            row = jnp.dot(hidden[...], wd[:, lanes], preferred_element_type=jnp.float32)
            row = row.astype(jnp.bfloat16).astype(jnp.float32) * route
            if e == 0:
                total[:, lanes] = row
            else:
                row = total[:, lanes] + row
                for k, out in enumerate(outs):
                    out[:, lanes] = row[k * block : (k + 1) * block].astype(out.dtype)


def ffn(shards, offsets, results, me, order, table, weights, holds):
    sizes = [s.shape[0] for s in shards]
    rows = sum(sizes)
    ff, width = weights[0].shape
    block = rows // results
    vmem = pl.BlockSpec(memory_space=pltpu.VMEM)
    smem = pl.BlockSpec(memory_space=pltpu.SMEM)
    hbm = pl.BlockSpec(memory_space=pl.ANY)
    chips = math.isqrt(order.shape[0])
    kept = 6 if holds else 0
    if holds:
        weights = [in_hbm(w) for w in weights]
    return pl.pallas_call(
        functools.partial(ffn_kernel, len(shards), results, sizes, offsets, chips, kept),
        out_shape=[jax.ShapeDtypeStruct((block, width), jnp.float32)] * results
        + [pltpu.VMEM(w.shape, w.dtype) for w in weights[:kept]],
        in_specs=[smem] * 2 + [vmem] * (len(shards) + 1) + [hbm if holds else vmem] * 6,
        out_specs=[vmem] * (results + kept),
        scratch_shapes=[
            pltpu.VMEM((rows, width), jnp.bfloat16),
            pltpu.VMEM((rows, ff), jnp.bfloat16),
            pltpu.VMEM((rows, width), jnp.float32),
        ]
        + [pltpu.SemaphoreType.DMA((6,))] * holds,
        compiler_params=pltpu.CompilerParams(vmem_limit_bytes=10 * 2**20),
        cost_estimate=pl.CostEstimate(
            flops=12 * rows * ff * width, bytes_accessed=12 * ff * width, transcendentals=2 * rows * ff
        ),
    )(me[None], order, *shards, table, *weights)


def place_kernel(slots, arrived_ref, counts_ref, owner_ref, me_ref, text_ref, out_ref):
    rows = text_ref.shape[0]
    devices = counts_ref.shape[0]
    held = arrived_ref.shape[0]
    mine = (owner_ref[...] == me_ref[0]).astype(jnp.int32)
    live = jnp.sum(counts_ref[...] * mine, axis=1, keepdims=True)
    total = jnp.sum(live)
    lane = lax.broadcasted_iota(jnp.int32, (devices, held), 1)
    holder = lane // slots
    which = lax.broadcasted_iota(jnp.int32, (devices, held), 0)
    own = jnp.sum(jnp.where(which == holder, live, 0), axis=0, keepdims=True)
    start = jnp.sum(jnp.where(which < holder, live, 0), axis=0, keepdims=True)
    offset = lane[:1] - holder[:1] * slots
    place = jnp.where(offset < own, start + offset, -1)
    row = lax.broadcasted_iota(jnp.int32, (rows, held), 0)
    pick = (row == place).astype(jnp.bfloat16)
    image = jnp.dot(pick, arrived_ref[...], preferred_element_type=jnp.float32).astype(jnp.bfloat16)
    position = lax.broadcasted_iota(jnp.int32, (rows, 1), 0)
    out_ref[...] = jnp.where(position < total, image, text_ref[...])


def place_images(arrived, counts, owner, me, text_block, slots):
    vmem = pl.BlockSpec(memory_space=pltpu.VMEM)
    return pl.pallas_call(
        functools.partial(place_kernel, slots),
        out_shape=jax.ShapeDtypeStruct(text_block.shape, text_block.dtype),
        in_specs=[vmem, vmem, vmem, pl.BlockSpec(memory_space=pltpu.SMEM), vmem],
        out_specs=vmem,
        compiler_params=pltpu.CompilerParams(vmem_limit_bytes=8 * 2**20),
    )(arrived, counts, owner[None, :], me[None], text_block)


def cut_kernel(below_ref, above_ref, first_ref, second_ref, sems):
    half = first_ref.shape[0]
    copies = [
        pltpu.make_async_copy(below_ref.at[pl.ds(0, half)], first_ref, sems.at[0]),
        pltpu.make_async_copy(above_ref.at[pl.ds(half, half)], second_ref, sems.at[1]),
    ]
    for copy in copies:
        copy.start()
    for copy in copies:
        copy.wait()


def cut(below, above):
    rows, width = below.shape
    vmem = pl.BlockSpec(memory_space=pltpu.VMEM)
    return pl.pallas_call(
        cut_kernel,
        out_shape=[jax.ShapeDtypeStruct((rows // 2, width), below.dtype)] * 2,
        in_specs=[pl.BlockSpec(memory_space=pl.ANY)] * 2,
        out_specs=[vmem] * 2,
        scratch_shapes=[pltpu.SemaphoreType.DMA((2,))],
        compiler_params=pltpu.CompilerParams(vmem_limit_bytes=2 * 2**20),
    )(below, above)


def merge_kernel(parts, *refs):
    for i in range(2):
        total, out = refs[i], refs[2 + 2 * parts + i]
        at = 0
        for came in refs[2 + i * parts : 2 + (i + 1) * parts]:
            part = pl.ds(at, came.shape[0])
            out[part, :] = (total[part, :] + came[...].astype(jnp.float32)).astype(out.dtype)
            at += came.shape[0]


def merge(above, below, up_parts, down_parts):
    parts = len(up_parts)
    vmem = pl.BlockSpec(memory_space=pltpu.VMEM)
    return pl.pallas_call(
        functools.partial(merge_kernel, parts),
        out_shape=[jax.ShapeDtypeStruct(above.shape, jnp.bfloat16)] * 2,
        in_specs=[vmem] * (2 + 2 * parts),
        out_specs=[vmem] * 2,
        compiler_params=pltpu.CompilerParams(vmem_limit_bytes=8 * 2**20),
    )(above, below, *up_parts, *down_parts)


def tie(*arrays):
    return lax.optimization_barrier(arrays)


def local(
    tokens,
    expert_picks,
    router,
    gate_weight,
    up_weight,
    down_weight,
    image_rows,
    image_counts,
    span_owner,
    text_rows,
):
    devices = lax.axis_size("expert")
    me = lax.axis_index("expert")
    width = tokens.shape[1]
    experts = gate_weight.shape[0] * devices
    slots = image_rows.shape[2]
    chips = devices // 2
    far = chips // 2
    ring = ring_of(chips)
    pos = {c: i for i, c in enumerate(ring)}

    def send(x, pairs):
        return lax.ppermute(x, "expert", pairs)

    up = [(2 * c + k, 2 * ring[(pos[c] + 1) % chips] + k) for c in range(chips) for k in range(2)]
    down = [(target, source) for source, target in up]
    sibling = [(d, d ^ 1) for d in range(devices)]

    own = [gate_weight[0].T, up_weight[0].T, down_weight[0]]
    others = [send(w, sibling) for w in own]

    order = jnp.array([ring[(pos[c] + offset) % chips] for c in range(chips) for offset in range(chips)], jnp.int32)

    def run(shards, offsets, results=None, holds=False):
        return ffn(shards, offsets, results or len(shards), me, order, table, weights, holds)

    def run_both(s):
        return run([below[s], above[s]], [chips - s, s])

    expert_picks, _ = tie(expert_picks, others[0])
    table = route_of(tokens, expert_picks, router)
    table = lax.all_to_all(table.reshape(devices, 8, -1), "expert", split_axis=0, concat_axis=0, tiled=True)
    table = table.reshape(8 * devices, -1)

    number = jnp.arange(devices, dtype=jnp.int32)
    span_of = jnp.sum(jnp.where(span_owner[:, None] == number[None, :], number[:, None], 0), axis=0)
    span_of, _ = tie(span_of, others[1])
    image_send = by_owner(image_rows[0], span_of)
    arrived = lax.all_to_all(image_send, "expert", split_axis=0, concat_axis=0, tiled=True)

    below, above = [tokens], [tokens]
    from_below, from_above = {}, {}
    for s in range(1, far):
        below.append(send(below[-1], up))
        above.append(send(above[-1], down))
        if s == far - 1:
            weights = own + others
            table, image_send = tie(table, image_send)
            from_below[s - 1], from_above[s - 1], *weights = run([below[s - 1], above[s - 1]], [chips - s + 1, s - 1], 2, True)
            below[s], above[s], from_below[s - 1], from_above[s - 1] = tie(
                below[s], above[s], from_below[s - 1], from_above[s - 1]
            )
        else:
            below[s], above[s], image_send = tie(below[s], above[s], image_send)

    first, second = cut(below[-1], above[-1])
    first, second = send(first, up), send(second, down)
    done = run([below[-1], above[-1]], [chips - far + 1, far - 1], 4)
    first, second, *done = tie(first, second, *done)

    def low(x):
        return x.astype(jnp.bfloat16)

    def add(mine, came):
        return low(mine + came.astype(jnp.float32))

    below_first, below_second, above_first, above_second = done
    short_up, short_down = send(low(above_first), up), send(low(below_second), down)
    far_first, far_second, result_first, result_second = run([first, second, tokens], [far, 0], 4)
    short_up, short_down, far_first, far_second = tie(short_up, short_down, far_first, far_second)
    long_up, long_down = send(low(far_second), up), send(low(far_first), down)
    from_below[1], from_above[1] = run_both(1)
    long_up, long_down, short_up, short_down, from_below[1], from_above[1] = tie(
        long_up, long_down, short_up, short_down, from_below[1], from_above[1]
    )
    long_up, long_down = send(add(above_second, long_up), up), send(add(below_first, long_down), down)
    going_up, going_down = merge(
        from_above[far - 2], from_below[far - 2], [short_up, long_up], [long_down, short_down]
    )
    for s in range(2, far - 2):
        if s not in from_below:
            from_below[s], from_above[s] = run_both(s)
    for s in range(far - 2, 0, -1):
        going_up, going_down = tie(send(going_up, up), send(going_down, down))
        if s > 1:
            going_up, going_down = merge(from_above[s - 1], from_below[s - 1], [going_up], [going_down])
    result = jnp.concatenate([result_first, result_second], axis=0)
    moe_out = low(result + going_up.astype(jnp.float32) + going_down.astype(jnp.float32))

    arrived = arrived.reshape(devices * slots, width)
    next_span = place_images(
        arrived, image_counts, span_owner, me, text_rows, slots
    )
    return (moe_out, next_span)


def solution(mesh):
    return jax.shard_map(
        local,
        mesh=mesh,
        in_specs=(
            P(("groups", "expert"), None),
            P(("groups", "expert"), None),
            P(),
            P("expert", None, None),
            P("expert", None, None),
            P("expert", None, None),
            P(("groups", "expert"), None, None, None),
            P("groups", None),
            P("groups"),
            P(("groups", "expert"), None),
        ),
        out_specs=(P(("groups", "expert"), None), P(("groups", "expert"), None)),
        check_vma=False,
    )
```

```python
import functools
import math

import jax
import jax.numpy as jnp
from jax import lax
from jax.experimental import pallas as pl
from jax.experimental.pallas import tpu as pltpu
from jax.sharding import PartitionSpec as P

route_scale = 2.446
NT = (((1,), (1,)), ((), ()))


def ring_of(chips):
    if chips <= 8:
        return list(range(0, chips, 2)) + list(range(chips - 1, 0, -2))
    return list(range(chips))


def route_kernel(picks_ref, router_hbm, tokens_hbm, out_ref, router_ref, tokens_ref, sems):
    experts = router_ref.shape[0]
    rows = tokens_ref.shape[0]
    take_tokens = pltpu.make_async_copy(tokens_hbm, tokens_ref, sems.at[0])
    take_router = pltpu.make_async_copy(router_hbm, router_ref, sems.at[1])
    take_tokens.start()
    take_router.start()
    take_tokens.wait()
    take_router.wait()
    logits = lax.dot_general(router_ref[...], tokens_ref[...], NT, preferred_element_type=jnp.float32)
    score = 1.0 / (1.0 + jnp.exp(-logits))
    expert = lax.broadcasted_iota(jnp.int32, (experts, rows), 0)
    picked = expert == picks_ref[0:1, :]
    for k in range(1, picks_ref.shape[0]):
        picked = jnp.logical_or(picked, expert == picks_ref[k : k + 1, :])
    total = jnp.sum(jnp.where(picked, score, 0.0), axis=0, keepdims=True)
    rest = jnp.where(picked, route_scale * score / total, 0.0)
    target = lax.broadcasted_iota(jnp.int32, (out_ref.shape[0], experts), 0)
    source = lax.broadcasted_iota(jnp.int32, (out_ref.shape[0], experts), 1)
    pick = jnp.logical_and(target % 8 < 2, source == ((target // 8) ^ (target % 8))).astype(jnp.bfloat16)
    lines = jnp.zeros(out_ref.shape, jnp.float32)
    for _ in range(3):
        part = rest.astype(jnp.bfloat16)
        rest = rest - part.astype(jnp.float32)
        lines = lines + jnp.dot(pick, part, preferred_element_type=jnp.float32)
    out_ref[...] = lines


def in_hbm(x):
    return pltpu.with_memory_space_constraint(x, pltpu.HBM)


def route_of(tokens, expert_picks, router):
    rows, width = tokens.shape
    experts = router.shape[1]
    vmem = pl.BlockSpec(memory_space=pltpu.VMEM)
    hbm = pl.BlockSpec(memory_space=pl.ANY)
    return pl.pallas_call(
        route_kernel,
        out_shape=jax.ShapeDtypeStruct((8 * experts, rows), jnp.float32),
        in_specs=[vmem, hbm, hbm],
        out_specs=vmem,
        scratch_shapes=[
            pltpu.VMEM((experts, width), router.dtype),
            pltpu.VMEM((rows, width), tokens.dtype),
            pltpu.SemaphoreType.DMA((2,)),
        ],
        compiler_params=pltpu.CompilerParams(vmem_limit_bytes=8 * 2**20),
    )(expert_picks.T, in_hbm(router.T), in_hbm(tokens))


def spans_kernel(me_ref, span_of_ref, rows_hbm, keep_ref, give_ref, sems):
    copies = []
    for c in range(keep_ref.shape[0]):
        for j, out in enumerate((keep_ref, give_ref)):
            owner = 2 * c + (me_ref[0] + j) % 2
            copies.append(pltpu.make_async_copy(rows_hbm.at[span_of_ref[owner]], out.at[c], sems.at[c, j]))
    for copy in copies:
        copy.start()
    for copy in copies:
        copy.wait()


def by_owner(me, image_rows, span_of):
    devices, slots, width = image_rows.shape
    smem = pl.BlockSpec(memory_space=pltpu.SMEM)
    return pl.pallas_call(
        spans_kernel,
        out_shape=[jax.ShapeDtypeStruct((devices // 2, slots, width), image_rows.dtype)] * 2,
        in_specs=[smem, smem, pl.BlockSpec(memory_space=pl.ANY)],
        out_specs=[pl.BlockSpec(memory_space=pltpu.VMEM)] * 2,
        scratch_shapes=[pltpu.SemaphoreType.DMA((devices // 2, 2))],
        compiler_params=pltpu.CompilerParams(vmem_limit_bytes=4 * 2**20),
    )(me[None], span_of, in_hbm(image_rows))


def ffn_kernel(count, results, sizes, offsets, chips, holds, me_ref, order_ref, *refs):
    shards = refs[:count]
    table = refs[count]
    weights = refs[count + 1 : count + 7]
    outs = refs[count + 7 : count + 7 + results]
    kept = refs[count + 7 + results : count + 7 + results + holds]
    x, hidden, total = refs[count + 7 + results + holds :][:3]
    copies = []
    if holds:
        sems = refs[-1]
        for i in range(6):
            copies.append(pltpu.make_async_copy(weights[i], kept[i], sems.at[i]))
            copies[i].start()
        weights = kept
    rows = sum(sizes)
    width = x.shape[1]
    block = rows // results
    at = 0
    for ref, m in zip(shards, sizes):
        x[pl.ds(at, m), :] = ref[...]
        at += m
    me = me_ref[0]
    tokens = rows // len(offsets)
    square = (tokens, tokens)
    eye = lax.broadcasted_iota(jnp.int32, square, 0) == lax.broadcasted_iota(jnp.int32, square, 1)
    routes = [[], []]
    for offset in offsets:
        source = 2 * order_ref[(me // 2) * chips + offset] + me % 2
        lines = table[pl.ds(pl.multiple_of(source * 8, 8), 8), :]
        for e in range(2):
            routes[e].append(jnp.sum(jnp.where(eye, lines[e : e + 1], 0.0), axis=1, keepdims=True))
    for e in range(2):
        wg, wu, wd = weights[3 * e : 3 * e + 3]
        route = jnp.concatenate(routes[e], axis=0)
        if holds:
            copies[3 * e].wait()
        gate = lax.dot_general(x[...], wg[...], NT, preferred_element_type=jnp.float32)
        if holds:
            copies[3 * e + 1].wait()
        upward = lax.dot_general(x[...], wu[...], NT, preferred_element_type=jnp.float32)
        hidden[...] = (gate / (1.0 + jnp.exp(-gate)) * upward).astype(jnp.bfloat16)
        if holds:
            copies[3 * e + 2].wait()
        for a in range(0, width, 512):
            lanes = pl.ds(a, 512)
            row = jnp.dot(hidden[...], wd[:, lanes], preferred_element_type=jnp.float32)
            row = row.astype(jnp.bfloat16).astype(jnp.float32) * route
            if e == 0:
                total[:, lanes] = row
            else:
                row = total[:, lanes] + row
                for k, out in enumerate(outs):
                    out[:, lanes] = row[k * block : (k + 1) * block].astype(out.dtype)


def ffn(shards, offsets, results, me, order, table, weights, holds):
    sizes = [s.shape[0] for s in shards]
    rows = sum(sizes)
    ff, width = weights[0].shape
    block = rows // results
    vmem = pl.BlockSpec(memory_space=pltpu.VMEM)
    smem = pl.BlockSpec(memory_space=pltpu.SMEM)
    hbm = pl.BlockSpec(memory_space=pl.ANY)
    chips = math.isqrt(order.shape[0])
    kept = 6 if holds else 0
    if holds:
        weights = [in_hbm(w) for w in weights]
    return pl.pallas_call(
        functools.partial(ffn_kernel, len(shards), results, sizes, offsets, chips, kept),
        out_shape=[jax.ShapeDtypeStruct((block, width), jnp.bfloat16)] * results
        + [pltpu.VMEM(w.shape, w.dtype) for w in weights[:kept]],
        in_specs=[smem] * 2 + [vmem] * (len(shards) + 1) + [hbm if holds else vmem] * 6,
        out_specs=[vmem] * (results + kept),
        scratch_shapes=[
            pltpu.VMEM((rows, width), jnp.bfloat16),
            pltpu.VMEM((rows, ff), jnp.bfloat16),
            pltpu.VMEM((rows, width), jnp.float32),
        ]
        + [pltpu.SemaphoreType.DMA((6,))] * holds,
        compiler_params=pltpu.CompilerParams(vmem_limit_bytes=10 * 2**20),
        cost_estimate=pl.CostEstimate(
            flops=12 * rows * ff * width, bytes_accessed=12 * ff * width, transcendentals=2 * rows * ff
        ),
    )(me[None], order, *shards, table, *weights)


def place_kernel(slots, arrived_ref, counts_ref, owner_ref, me_ref, text_ref, out_ref):
    rows = text_ref.shape[0]
    devices = counts_ref.shape[0]
    held = arrived_ref.shape[0]
    mine = (owner_ref[...] == me_ref[0]).astype(jnp.int32)
    live = jnp.sum(counts_ref[...] * mine, axis=1, keepdims=True)
    total = jnp.sum(live)
    lane = lax.broadcasted_iota(jnp.int32, (devices, held), 1)
    group = lane // slots
    holder = 2 * (group // 2) + (me_ref[0] + group) % 2
    which = lax.broadcasted_iota(jnp.int32, (devices, held), 0)
    own = jnp.sum(jnp.where(which == holder, live, 0), axis=0, keepdims=True)
    start = jnp.sum(jnp.where(which < holder, live, 0), axis=0, keepdims=True)
    offset = lane[:1] - group[:1] * slots
    place = jnp.where(offset < own, start + offset, -1)
    row = lax.broadcasted_iota(jnp.int32, (rows, held), 0)
    pick = (row == place).astype(jnp.bfloat16)
    image = jnp.dot(pick, arrived_ref[...], preferred_element_type=jnp.float32).astype(jnp.bfloat16)
    position = lax.broadcasted_iota(jnp.int32, (rows, 1), 0)
    out_ref[...] = jnp.where(position < total, image, text_ref[...])


def place_images(arrived, counts, owner, me, text_block, slots):
    vmem = pl.BlockSpec(memory_space=pltpu.VMEM)
    return pl.pallas_call(
        functools.partial(place_kernel, slots),
        out_shape=jax.ShapeDtypeStruct(text_block.shape, text_block.dtype),
        in_specs=[vmem, vmem, vmem, pl.BlockSpec(memory_space=pltpu.SMEM), vmem],
        out_specs=vmem,
        compiler_params=pltpu.CompilerParams(vmem_limit_bytes=8 * 2**20),
    )(arrived, counts, owner[None, :], me[None], text_block)


def cut_kernel(below_ref, above_ref, first_ref, second_ref, sems):
    half = first_ref.shape[0]
    copies = [
        pltpu.make_async_copy(below_ref.at[pl.ds(0, half)], first_ref, sems.at[0]),
        pltpu.make_async_copy(above_ref.at[pl.ds(half, half)], second_ref, sems.at[1]),
    ]
    for copy in copies:
        copy.start()
    for copy in copies:
        copy.wait()


def cut(below, above):
    rows, width = below.shape
    vmem = pl.BlockSpec(memory_space=pltpu.VMEM)
    return pl.pallas_call(
        cut_kernel,
        out_shape=[jax.ShapeDtypeStruct((rows // 2, width), below.dtype)] * 2,
        in_specs=[pl.BlockSpec(memory_space=pl.ANY)] * 2,
        out_specs=[vmem] * 2,
        scratch_shapes=[pltpu.SemaphoreType.DMA((2,))],
        compiler_params=pltpu.CompilerParams(vmem_limit_bytes=2 * 2**20),
    )(below, above)


def merge_kernel(parts, *refs):
    for i in range(2):
        total, out = refs[i], refs[2 + 2 * parts + i]
        at = 0
        for came in refs[2 + i * parts : 2 + (i + 1) * parts]:
            part = pl.ds(at, came.shape[0])
            out[part, :] = (total[part, :].astype(jnp.float32) + came[...].astype(jnp.float32)).astype(out.dtype)
            at += came.shape[0]


def merge(above, below, up_parts, down_parts):
    parts = len(up_parts)
    vmem = pl.BlockSpec(memory_space=pltpu.VMEM)
    return pl.pallas_call(
        functools.partial(merge_kernel, parts),
        out_shape=[jax.ShapeDtypeStruct(above.shape, jnp.bfloat16)] * 2,
        in_specs=[vmem] * (2 + 2 * parts),
        out_specs=[vmem] * 2,
        compiler_params=pltpu.CompilerParams(vmem_limit_bytes=8 * 2**20),
    )(above, below, *up_parts, *down_parts)


def finish_kernel(first_ref, second_ref, up_ref, down_ref, out_ref):
    half = first_ref.shape[0]
    for i, mine in enumerate((first_ref, second_ref)):
        part = pl.ds(i * half, half)
        total = mine[...].astype(jnp.float32) + up_ref[part, :].astype(jnp.float32)
        out_ref[part, :] = (total + down_ref[part, :].astype(jnp.float32)).astype(out_ref.dtype)


def finish(first, second, came_up, came_down):
    vmem = pl.BlockSpec(memory_space=pltpu.VMEM)
    return pl.pallas_call(
        finish_kernel,
        out_shape=jax.ShapeDtypeStruct(came_up.shape, came_up.dtype),
        in_specs=[vmem] * 4,
        out_specs=vmem,
        compiler_params=pltpu.CompilerParams(vmem_limit_bytes=8 * 2**20),
    )(first, second, came_up, came_down)


def tie(*arrays):
    return lax.optimization_barrier(arrays)


def local(
    tokens,
    expert_picks,
    router,
    gate_weight,
    up_weight,
    down_weight,
    image_rows,
    image_counts,
    span_owner,
    text_rows,
):
    devices = lax.axis_size("expert")
    me = lax.axis_index("expert")
    width = tokens.shape[1]
    experts = gate_weight.shape[0] * devices
    slots = image_rows.shape[2]
    chips = devices // 2
    far = chips // 2
    ring = ring_of(chips)
    pos = {c: i for i, c in enumerate(ring)}

    def send(x, pairs):
        return lax.ppermute(x, "expert", pairs)

    up = [(2 * c + k, 2 * ring[(pos[c] + 1) % chips] + k) for c in range(chips) for k in range(2)]
    down = [(target, source) for source, target in up]
    sibling = [(d, d ^ 1) for d in range(devices)]

    own = [gate_weight[0].T, up_weight[0].T, down_weight[0]]
    others = [send(w, sibling) for w in own]

    order = jnp.array([ring[(pos[c] + offset) % chips] for c in range(chips) for offset in range(chips)], jnp.int32)

    def run(shards, offsets, results=None, holds=False):
        return ffn(shards, offsets, results or len(shards), me, order, table, weights, holds)

    def run_both(s):
        return run([below[s], above[s]], [chips - s, s])

    parity = [[2 * c + k for c in range(chips)] for k in range(2)]

    def exchange(x):
        return lax.all_to_all(x, "expert", split_axis=0, concat_axis=0, tiled=True, axis_index_groups=parity)

    expert_picks, _ = tie(expert_picks, others[0])
    table = route_of(tokens, expert_picks, router)
    table = lax.all_to_all(table.reshape(devices, 8, -1), "expert", split_axis=0, concat_axis=0, tiled=True)
    table = table.reshape(8 * devices, -1)

    number = jnp.arange(devices, dtype=jnp.int32)
    span_of = jnp.sum(jnp.where(span_owner[:, None] == number[None, :], number[:, None], 0), axis=0)
    span_of, _ = tie(span_of, others[1])
    keep, give = by_owner(me, image_rows[0], span_of)

    below, above = [tokens], [tokens]
    from_below, from_above = {}, {}
    for s in range(1, far):
        below.append(send(below[-1], up))
        above.append(send(above[-1], down))
        if s == far - 1:
            weights = own + others
            table, image_send = tie(table, image_send)
            from_below[s - 1], from_above[s - 1], *weights = run([below[s - 1], above[s - 1]], [chips - s + 1, s - 1], 2, True)
            below[s], above[s], from_below[s - 1], from_above[s - 1] = tie(
                below[s], above[s], from_below[s - 1], from_above[s - 1]
            )
        else:
            if s == 1:
                below[s], above[s], keep, give = tie(below[s], above[s], keep, give)
                image_send = jnp.stack([keep, send(give, sibling)], axis=1)
            else:
                below[s], above[s], image_send = tie(below[s], above[s], image_send)

    arrived = exchange(image_send)

    first, second = cut(below[-1], above[-1])
    first, second = send(first, up), send(second, down)
    done = run([below[-1], above[-1]], [chips - far + 1, far - 1], 4)
    first, second, *done = tie(first, second, *done)

    def add(mine, *came):
        return sum([c.astype(jnp.float32) for c in came], mine.astype(jnp.float32)).astype(jnp.bfloat16)

    below_first, below_second, above_first, above_second = done
    short_up, short_down = send(above_first, up), send(below_second, down)
    far_first, far_second, result_first, result_second = run([first, second, tokens], [far, 0], 4)
    short_up, short_down, far_first, far_second = tie(short_up, short_down, far_first, far_second)
    long_up, long_down = send(far_second, up), send(far_first, down)
    from_below[1], from_above[1] = run_both(1)
    long_up, long_down, short_up, short_down, from_below[1], from_above[1] = tie(
        long_up, long_down, short_up, short_down, from_below[1], from_above[1]
    )
    long_up, long_down = send(add(above_second, long_up), up), send(add(below_first, long_down), down)
    going_up, going_down = merge(
        from_above[far - 2], from_below[far - 2], [short_up, long_up], [long_down, short_down]
    )
    for s in range(2, far - 2):
        if s not in from_below:
            from_below[s], from_above[s] = run_both(s)
    for s in range(far - 2, 0, -1):
        going_up, going_down = tie(send(going_up, up), send(going_down, down))
        if s > 1:
            going_up, going_down = merge(from_above[s - 1], from_below[s - 1], [going_up], [going_down])
    moe_out = finish(in_hbm(result_first), in_hbm(result_second), going_up, going_down)

    arrived = arrived.reshape(devices * slots, width)
    next_span = place_images(
        arrived, image_counts, span_owner, me, text_rows, slots
    )
    return (moe_out, next_span)


def solution(mesh):
    return jax.shard_map(
        local,
        mesh=mesh,
        in_specs=(
            P(("groups", "expert"), None),
            P(("groups", "expert"), None),
            P(),
            P("expert", None, None),
            P("expert", None, None),
            P("expert", None, None),
            P(("groups", "expert"), None, None, None),
            P("groups", None),
            P("groups"),
            P(("groups", "expert"), None),
        ),
        out_specs=(P(("groups", "expert"), None), P(("groups", "expert"), None)),
        check_vma=False,
    )
```

```python
import functools
import math

import jax
import jax.numpy as jnp
from jax import lax
from jax.experimental import pallas as pl
from jax.experimental.pallas import tpu as pltpu
from jax.sharding import PartitionSpec as P

route_scale = 2.446
NT = (((1,), (1,)), ((), ()))


def ring_of(chips):
    if chips <= 8:
        return list(range(0, chips, 2)) + list(range(chips - 1, 0, -2))
    return list(range(chips))


def route_kernel(picks_ref, router_hbm, tokens_hbm, out_ref, router_ref, tokens_ref, sems):
    experts = router_ref.shape[0]
    rows = tokens_ref.shape[0]
    take_tokens = pltpu.make_async_copy(tokens_hbm, tokens_ref, sems.at[0])
    take_router = pltpu.make_async_copy(router_hbm, router_ref, sems.at[1])
    take_tokens.start()
    take_router.start()
    take_tokens.wait()
    take_router.wait()
    logits = lax.dot_general(router_ref[...], tokens_ref[...], NT, preferred_element_type=jnp.float32)
    score = 1.0 / (1.0 + jnp.exp(-logits))
    expert = lax.broadcasted_iota(jnp.int32, (experts, rows), 0)
    picked = expert == picks_ref[0:1, :]
    for k in range(1, picks_ref.shape[0]):
        picked = jnp.logical_or(picked, expert == picks_ref[k : k + 1, :])
    total = jnp.sum(jnp.where(picked, score, 0.0), axis=0, keepdims=True)
    rest = jnp.where(picked, route_scale * score / total, 0.0)
    target = lax.broadcasted_iota(jnp.int32, (out_ref.shape[0], experts), 0)
    source = lax.broadcasted_iota(jnp.int32, (out_ref.shape[0], experts), 1)
    pick = jnp.logical_and(target % 8 < 2, source == ((target // 8) ^ (target % 8))).astype(jnp.bfloat16)
    lines = jnp.zeros(out_ref.shape, jnp.float32)
    for _ in range(3):
        part = rest.astype(jnp.bfloat16)
        rest = rest - part.astype(jnp.float32)
        lines = lines + jnp.dot(pick, part, preferred_element_type=jnp.float32)
    out_ref[...] = lines


def in_hbm(x):
    return pltpu.with_memory_space_constraint(x, pltpu.HBM)


def route_of(tokens, expert_picks, router):
    rows, width = tokens.shape
    experts = router.shape[1]
    vmem = pl.BlockSpec(memory_space=pltpu.VMEM)
    hbm = pl.BlockSpec(memory_space=pl.ANY)
    return pl.pallas_call(
        route_kernel,
        out_shape=jax.ShapeDtypeStruct((8 * experts, rows), jnp.float32),
        in_specs=[vmem, hbm, hbm],
        out_specs=vmem,
        scratch_shapes=[
            pltpu.VMEM((experts, width), router.dtype),
            pltpu.VMEM((rows, width), tokens.dtype),
            pltpu.SemaphoreType.DMA((2,)),
        ],
        compiler_params=pltpu.CompilerParams(vmem_limit_bytes=8 * 2**20),
    )(expert_picks.T, in_hbm(router.T), in_hbm(tokens))


def spans_kernel(me_ref, span_of_ref, rows_hbm, keep_ref, give_ref, sems):
    copies = []
    for c in range(keep_ref.shape[0]):
        for j, out in enumerate((keep_ref, give_ref)):
            owner = 2 * c + (me_ref[0] + j) % 2
            copies.append(pltpu.make_async_copy(rows_hbm.at[span_of_ref[owner]], out.at[c], sems.at[c, j]))
    for copy in copies:
        copy.start()
    for copy in copies:
        copy.wait()


def by_owner(me, image_rows, span_of):
    devices, slots, width = image_rows.shape
    smem = pl.BlockSpec(memory_space=pltpu.SMEM)
    return pl.pallas_call(
        spans_kernel,
        out_shape=[jax.ShapeDtypeStruct((devices // 2, slots, width), image_rows.dtype)] * 2,
        in_specs=[smem, smem, pl.BlockSpec(memory_space=pl.ANY)],
        out_specs=[pl.BlockSpec(memory_space=pltpu.VMEM)] * 2,
        scratch_shapes=[pltpu.SemaphoreType.DMA((devices // 2, 2))],
        compiler_params=pltpu.CompilerParams(vmem_limit_bytes=4 * 2**20),
    )(me[None], span_of, in_hbm(image_rows))


def pair_kernel(kept_ref, other_ref, out_ref):
    for c in range(out_ref.shape[0]):
        out_ref[c, 0] = kept_ref[c]
        out_ref[c, 1] = other_ref[c]


def pair(kept, other):
    chips, slots, width = kept.shape
    vmem = pl.BlockSpec(memory_space=pltpu.VMEM)
    return pl.pallas_call(
        pair_kernel,
        out_shape=jax.ShapeDtypeStruct((chips, 2, slots, width), kept.dtype),
        in_specs=[vmem] * 2,
        out_specs=vmem,
        compiler_params=pltpu.CompilerParams(vmem_limit_bytes=8 * 2**20),
    )(kept, other)


def ffn_kernel(count, results, sizes, offsets, chips, holds, me_ref, order_ref, *refs):
    shards = refs[:count]
    table = refs[count]
    weights = refs[count + 1 : count + 7]
    outs = refs[count + 7 : count + 7 + results]
    kept = refs[count + 7 + results : count + 7 + results + holds]
    x, hidden, total = refs[count + 7 + results + holds :][:3]
    copies = []
    if holds:
        sems = refs[-1]
        for i in range(6):
            copies.append(pltpu.make_async_copy(weights[i], kept[i], sems.at[i]))
            copies[i].start()
        weights = kept
    rows = sum(sizes)
    width = x.shape[1]
    block = rows // results
    at = 0
    for ref, m in zip(shards, sizes):
        x[pl.ds(at, m), :] = ref[...]
        at += m
    me = me_ref[0]
    tokens = rows // len(offsets)
    square = (tokens, tokens)
    eye = lax.broadcasted_iota(jnp.int32, square, 0) == lax.broadcasted_iota(jnp.int32, square, 1)
    routes = [[], []]
    for offset in offsets:
        source = 2 * order_ref[(me // 2) * chips + offset] + me % 2
        lines = table[pl.ds(pl.multiple_of(source * 8, 8), 8), :]
        for e in range(2):
            routes[e].append(jnp.sum(jnp.where(eye, lines[e : e + 1], 0.0), axis=1, keepdims=True))
    for e in range(2):
        wg, wu, wd = weights[3 * e : 3 * e + 3]
        route = jnp.concatenate(routes[e], axis=0)
        if holds:
            copies[3 * e].wait()
        gate = lax.dot_general(x[...], wg[...], NT, preferred_element_type=jnp.float32)
        if holds:
            copies[3 * e + 1].wait()
        upward = lax.dot_general(x[...], wu[...], NT, preferred_element_type=jnp.float32)
        hidden[...] = (gate / (1.0 + jnp.exp(-gate)) * upward).astype(jnp.bfloat16)
        if holds:
            copies[3 * e + 2].wait()
        for a in range(0, width, 512):
            lanes = pl.ds(a, 512)
            row = jnp.dot(hidden[...], wd[:, lanes], preferred_element_type=jnp.float32)
            row = row.astype(jnp.bfloat16).astype(jnp.float32) * route
            if e == 0:
                total[:, lanes] = row
            else:
                row = total[:, lanes] + row
                for k, out in enumerate(outs):
                    out[:, lanes] = row[k * block : (k + 1) * block].astype(out.dtype)


def ffn(shards, offsets, results, me, order, table, weights, holds):
    sizes = [s.shape[0] for s in shards]
    rows = sum(sizes)
    ff, width = weights[0].shape
    block = rows // results
    vmem = pl.BlockSpec(memory_space=pltpu.VMEM)
    smem = pl.BlockSpec(memory_space=pltpu.SMEM)
    hbm = pl.BlockSpec(memory_space=pl.ANY)
    chips = math.isqrt(order.shape[0])
    kept = 6 if holds else 0
    if holds:
        weights = [in_hbm(w) for w in weights]
    return pl.pallas_call(
        functools.partial(ffn_kernel, len(shards), results, sizes, offsets, chips, kept),
        out_shape=[jax.ShapeDtypeStruct((block, width), jnp.bfloat16)] * results
        + [pltpu.VMEM(w.shape, w.dtype) for w in weights[:kept]],
        in_specs=[smem] * 2 + [vmem] * (len(shards) + 1) + [hbm if holds else vmem] * 6,
        out_specs=[vmem] * (results + kept),
        scratch_shapes=[
            pltpu.VMEM((rows, width), jnp.bfloat16),
            pltpu.VMEM((rows, ff), jnp.bfloat16),
            pltpu.VMEM((rows, width), jnp.float32),
        ]
        + [pltpu.SemaphoreType.DMA((6,))] * holds,
        compiler_params=pltpu.CompilerParams(vmem_limit_bytes=10 * 2**20),
        cost_estimate=pl.CostEstimate(
            flops=12 * rows * ff * width, bytes_accessed=12 * ff * width, transcendentals=2 * rows * ff
        ),
    )(me[None], order, *shards, table, *weights)


def place_kernel(slots, arrived_ref, counts_ref, owner_ref, me_ref, text_ref, first_ref, second_ref, out_ref, near_ref):
    half = first_ref.shape[0]
    near_ref[:half, :] = first_ref[...]
    near_ref[half:, :] = second_ref[...]
    rows = text_ref.shape[0]
    devices = counts_ref.shape[0]
    held = arrived_ref.shape[0]
    mine = (owner_ref[...] == me_ref[0]).astype(jnp.int32)
    live = jnp.sum(counts_ref[...] * mine, axis=1, keepdims=True)
    total = jnp.sum(live)
    lane = lax.broadcasted_iota(jnp.int32, (devices, held), 1)
    group = lane // slots
    holder = 2 * (group // 2) + (me_ref[0] + group) % 2
    which = lax.broadcasted_iota(jnp.int32, (devices, held), 0)
    own = jnp.sum(jnp.where(which == holder, live, 0), axis=0, keepdims=True)
    start = jnp.sum(jnp.where(which < holder, live, 0), axis=0, keepdims=True)
    offset = lane[:1] - group[:1] * slots
    place = jnp.where(offset < own, start + offset, -1)
    row = lax.broadcasted_iota(jnp.int32, (rows, held), 0)
    pick = (row == place).astype(jnp.bfloat16)
    image = jnp.dot(pick, arrived_ref[...], preferred_element_type=jnp.float32).astype(jnp.bfloat16)
    position = lax.broadcasted_iota(jnp.int32, (rows, 1), 0)
    out_ref[...] = jnp.where(position < total, image, text_ref[...])


def place_images(arrived, counts, owner, me, text_block, slots, first, second):
    vmem = pl.BlockSpec(memory_space=pltpu.VMEM)
    return pl.pallas_call(
        functools.partial(place_kernel, slots),
        out_shape=[
            jax.ShapeDtypeStruct(text_block.shape, text_block.dtype),
            pltpu.VMEM(text_block.shape, first.dtype),
        ],
        in_specs=[vmem, vmem, vmem, pl.BlockSpec(memory_space=pltpu.SMEM), vmem, vmem, vmem],
        out_specs=[vmem] * 2,
        compiler_params=pltpu.CompilerParams(vmem_limit_bytes=8 * 2**20),
    )(arrived, counts, owner[None, :], me[None], text_block, first, second)


def cut_kernel(below_ref, above_ref, first_ref, second_ref, sems):
    half = first_ref.shape[0]
    copies = [
        pltpu.make_async_copy(below_ref.at[pl.ds(0, half)], first_ref, sems.at[0]),
        pltpu.make_async_copy(above_ref.at[pl.ds(half, half)], second_ref, sems.at[1]),
    ]
    for copy in copies:
        copy.start()
    for copy in copies:
        copy.wait()


def cut(below, above):
    rows, width = below.shape
    vmem = pl.BlockSpec(memory_space=pltpu.VMEM)
    return pl.pallas_call(
        cut_kernel,
        out_shape=[jax.ShapeDtypeStruct((rows // 2, width), below.dtype)] * 2,
        in_specs=[pl.BlockSpec(memory_space=pl.ANY)] * 2,
        out_specs=[vmem] * 2,
        scratch_shapes=[pltpu.SemaphoreType.DMA((2,))],
        compiler_params=pltpu.CompilerParams(vmem_limit_bytes=2 * 2**20),
    )(below, above)


def merge_kernel(parts, *refs):
    for i in range(2):
        total, out = refs[i], refs[2 + 2 * parts + i]
        at = 0
        for came in refs[2 + i * parts : 2 + (i + 1) * parts]:
            part = pl.ds(at, came.shape[0])
            out[part, :] = (total[part, :].astype(jnp.float32) + came[...].astype(jnp.float32)).astype(out.dtype)
            at += came.shape[0]


def merge(above, below, up_parts, down_parts):
    parts = len(up_parts)
    vmem = pl.BlockSpec(memory_space=pltpu.VMEM)
    return pl.pallas_call(
        functools.partial(merge_kernel, parts),
        out_shape=[jax.ShapeDtypeStruct(above.shape, jnp.bfloat16)] * 2,
        in_specs=[vmem] * (2 + 2 * parts),
        out_specs=[vmem] * 2,
        compiler_params=pltpu.CompilerParams(vmem_limit_bytes=8 * 2**20),
    )(above, below, *up_parts, *down_parts)


def finish_kernel(near_ref, up_ref, down_ref, out_ref):
    total = near_ref[...].astype(jnp.float32) + up_ref[...].astype(jnp.float32)
    out_ref[...] = (total + down_ref[...].astype(jnp.float32)).astype(out_ref.dtype)


def finish(near, came_up, came_down):
    vmem = pl.BlockSpec(memory_space=pltpu.VMEM)
    return pl.pallas_call(
        finish_kernel,
        out_shape=jax.ShapeDtypeStruct(near.shape, near.dtype),
        in_specs=[vmem] * 3,
        out_specs=vmem,
        compiler_params=pltpu.CompilerParams(vmem_limit_bytes=8 * 2**20),
    )(near, came_up, came_down)


def tie(*arrays):
    return lax.optimization_barrier(arrays)


def local(
    tokens,
    expert_picks,
    router,
    gate_weight,
    up_weight,
    down_weight,
    image_rows,
    image_counts,
    span_owner,
    text_rows,
):
    devices = lax.axis_size("expert")
    me = lax.axis_index("expert")
    width = tokens.shape[1]
    experts = gate_weight.shape[0] * devices
    slots = image_rows.shape[2]
    chips = devices // 2
    far = chips // 2
    ring = ring_of(chips)
    pos = {c: i for i, c in enumerate(ring)}

    def send(x, pairs):
        return lax.ppermute(x, "expert", pairs)

    up = [(2 * c + k, 2 * ring[(pos[c] + 1) % chips] + k) for c in range(chips) for k in range(2)]
    down = [(target, source) for source, target in up]
    sibling = [(d, d ^ 1) for d in range(devices)]

    own = [gate_weight[0].T, up_weight[0].T, down_weight[0]]
    others = [send(w, sibling) for w in own]

    order = jnp.array([ring[(pos[c] + offset) % chips] for c in range(chips) for offset in range(chips)], jnp.int32)

    def run(shards, offsets, results=None, holds=False):
        return ffn(shards, offsets, results or len(shards), me, order, table, weights, holds)

    def run_both(s):
        return run([below[s], above[s]], [chips - s, s])

    parity = [[2 * c + k for c in range(chips)] for k in range(2)]

    def exchange(x):
        return lax.all_to_all(x, "expert", split_axis=0, concat_axis=0, tiled=True, axis_index_groups=parity)

    expert_picks, _ = tie(expert_picks, others[0])
    table = route_of(tokens, expert_picks, router)
    table = lax.all_to_all(table.reshape(devices, 8, -1), "expert", split_axis=0, concat_axis=0, tiled=True)
    table = table.reshape(8 * devices, -1)

    number = jnp.arange(devices, dtype=jnp.int32)
    span_of = jnp.sum(jnp.where(span_owner[:, None] == number[None, :], number[:, None], 0), axis=0)
    span_of, _ = tie(span_of, others[1])
    keep, give = by_owner(me, image_rows[0], span_of)

    below, above = [tokens], [tokens]
    from_below, from_above = {}, {}
    for s in range(1, far):
        below.append(send(below[-1], up))
        above.append(send(above[-1], down))
        if s == far - 1:
            weights = own + others
            table, image_send = tie(table, image_send)
            from_below[s - 1], from_above[s - 1], *weights = run([below[s - 1], above[s - 1]], [chips - s + 1, s - 1], 2, True)
            below[s], above[s], from_below[s - 1], from_above[s - 1] = tie(
                below[s], above[s], from_below[s - 1], from_above[s - 1]
            )
        else:
            if s == 1:
                below[s], above[s], keep, give = tie(below[s], above[s], keep, give)
                image_send = pair(keep, send(give, sibling))
            else:
                below[s], above[s], image_send = tie(below[s], above[s], image_send)

    arrived = exchange(image_send)

    first, second = cut(below[-1], above[-1])
    first, second = send(first, up), send(second, down)
    done = run([below[-1], above[-1]], [chips - far + 1, far - 1], 4)
    first, second, *done = tie(first, second, *done)

    def add(mine, *came):
        return sum([c.astype(jnp.float32) for c in came], mine.astype(jnp.float32)).astype(jnp.bfloat16)

    below_first, below_second, above_first, above_second = done
    short_up, short_down = send(above_first, up), send(below_second, down)
    far_first, far_second, result_first, result_second = run([first, second, tokens], [far, 0], 4)
    short_up, short_down, far_first, far_second = tie(short_up, short_down, far_first, far_second)
    long_up, long_down = send(far_second, up), send(far_first, down)
    from_below[1], from_above[1] = run_both(1)
    long_up, long_down, short_up, short_down, from_below[1], from_above[1] = tie(
        long_up, long_down, short_up, short_down, from_below[1], from_above[1]
    )
    long_up, long_down = send(add(above_second, long_up), up), send(add(below_first, long_down), down)
    going_up, going_down = merge(
        from_above[far - 2], from_below[far - 2], [short_up, long_up], [long_down, short_down]
    )
    for s in range(2, far - 2):
        if s not in from_below:
            from_below[s], from_above[s] = run_both(s)
    for s in range(far - 2, 0, -1):
        going_up, going_down = tie(send(going_up, up), send(going_down, down))
        if s > 1:
            going_up, going_down = merge(from_above[s - 1], from_below[s - 1], [going_up], [going_down])
    arrived = arrived.reshape(devices * slots, width)
    next_span, near = place_images(
        arrived, image_counts, span_owner, me, text_rows, slots, result_first, result_second
    )
    moe_out = finish(near, going_up, going_down)
    return (moe_out, next_span)


def solution(mesh):
    return jax.shard_map(
        local,
        mesh=mesh,
        in_specs=(
            P(("groups", "expert"), None),
            P(("groups", "expert"), None),
            P(),
            P("expert", None, None),
            P("expert", None, None),
            P("expert", None, None),
            P(("groups", "expert"), None, None, None),
            P("groups", None),
            P("groups"),
            P(("groups", "expert"), None),
        ),
        out_specs=(P(("groups", "expert"), None), P(("groups", "expert"), None)),
        check_vma=False,
    )
```

```python
import functools

import jax
import jax.numpy as jnp
from jax import lax
from jax.experimental import pallas as pl
from jax.experimental.pallas import tpu as pltpu
from jax.sharding import PartitionSpec as P

route_scale = 2.446
NT = (((1,), (1,)), ((), ()))


def folded(chips):
    return chips <= 8


def chip_at(place, chips):
    if not folded(chips):
        return place
    return jnp.where(place < chips // 2, 2 * place, 2 * chips - 1 - 2 * place)


def place_of(chip, chips):
    if not folded(chips):
        return chip
    return jnp.where(chip % 2 == 0, chip // 2, (2 * chips - 1 - chip) // 2)


def ring_of(chips):
    if not folded(chips):
        return list(range(chips))
    return list(range(0, chips, 2)) + list(range(chips - 1, 0, -2))


def route_kernel(picks_ref, router_hbm, tokens_hbm, out_ref, router_ref, tokens_ref, sems):
    experts = router_ref.shape[0]
    rows = tokens_ref.shape[0]
    take_tokens = pltpu.make_async_copy(tokens_hbm, tokens_ref, sems.at[0])
    take_router = pltpu.make_async_copy(router_hbm, router_ref, sems.at[1])
    take_tokens.start()
    take_router.start()
    take_tokens.wait()
    take_router.wait()
    logits = lax.dot_general(router_ref[...], tokens_ref[...], NT, preferred_element_type=jnp.float32)
    score = 1.0 / (1.0 + jnp.exp(-logits))
    expert = lax.broadcasted_iota(jnp.int32, (experts, rows), 0)
    picked = expert == picks_ref[0:1, :]
    for k in range(1, picks_ref.shape[0]):
        picked = jnp.logical_or(picked, expert == picks_ref[k : k + 1, :])
    total = jnp.sum(jnp.where(picked, score, 0.0), axis=0, keepdims=True)
    rest = jnp.where(picked, route_scale * score / total, 0.0)
    target = lax.broadcasted_iota(jnp.int32, (out_ref.shape[0], experts), 0)
    source = lax.broadcasted_iota(jnp.int32, (out_ref.shape[0], experts), 1)
    pick = jnp.logical_and(target % 8 < 2, source == ((target // 8) ^ (target % 8))).astype(jnp.bfloat16)
    lines = jnp.zeros(out_ref.shape, jnp.float32)
    for _ in range(3):
        part = rest.astype(jnp.bfloat16)
        rest = rest - part.astype(jnp.float32)
        lines = lines + jnp.dot(pick, part, preferred_element_type=jnp.float32)
    out_ref[...] = lines


def in_hbm(x):
    return pltpu.with_memory_space_constraint(x, pltpu.HBM)


def route_of(tokens, expert_picks, router):
    rows, width = tokens.shape
    experts = router.shape[1]
    vmem = pl.BlockSpec(memory_space=pltpu.VMEM)
    hbm = pl.BlockSpec(memory_space=pl.ANY)
    return pl.pallas_call(
        route_kernel,
        out_shape=jax.ShapeDtypeStruct((8 * experts, rows), jnp.float32),
        in_specs=[vmem, hbm, hbm],
        out_specs=vmem,
        scratch_shapes=[
            pltpu.VMEM((experts, width), router.dtype),
            pltpu.VMEM((rows, width), tokens.dtype),
            pltpu.SemaphoreType.DMA((2,)),
        ],
        compiler_params=pltpu.CompilerParams(vmem_limit_bytes=8 * 2**20),
    )(expert_picks.T, in_hbm(router.T), in_hbm(tokens))


def spans_kernel(me_ref, span_of_ref, rows_hbm, keep_ref, give_ref, sems):
    copies = []
    for c in range(keep_ref.shape[0]):
        for j, out in enumerate((keep_ref, give_ref)):
            owner = 2 * c + (me_ref[0] + j) % 2
            copies.append(pltpu.make_async_copy(rows_hbm.at[span_of_ref[owner]], out.at[c], sems.at[c, j]))
    for copy in copies:
        copy.start()
    for copy in copies:
        copy.wait()


def by_owner(me, image_rows, span_of):
    devices, slots, width = image_rows.shape
    smem = pl.BlockSpec(memory_space=pltpu.SMEM)
    return pl.pallas_call(
        spans_kernel,
        out_shape=[jax.ShapeDtypeStruct((devices // 2, slots, width), image_rows.dtype)] * 2,
        in_specs=[smem, smem, pl.BlockSpec(memory_space=pl.ANY)],
        out_specs=[pl.BlockSpec(memory_space=pltpu.VMEM)] * 2,
        scratch_shapes=[pltpu.SemaphoreType.DMA((devices // 2, 2))],
        compiler_params=pltpu.CompilerParams(vmem_limit_bytes=4 * 2**20),
    )(me[None], span_of, in_hbm(image_rows))


def pair_kernel(kept_ref, other_ref, out_ref):
    for c in range(out_ref.shape[0]):
        out_ref[c, 0] = kept_ref[c]
        out_ref[c, 1] = other_ref[c]


def pair(kept, other):
    chips, slots, width = kept.shape
    vmem = pl.BlockSpec(memory_space=pltpu.VMEM)
    return pl.pallas_call(
        pair_kernel,
        out_shape=jax.ShapeDtypeStruct((chips, 2, slots, width), kept.dtype),
        in_specs=[vmem] * 2,
        out_specs=vmem,
        compiler_params=pltpu.CompilerParams(vmem_limit_bytes=8 * 2**20),
    )(kept, other)


def ffn_kernel(count, results, sizes, offsets, chips, holds, *refs):
    shards = refs[:count]
    table = refs[count]
    weights = refs[count + 1 : count + 7]
    outs = refs[count + 7 : count + 7 + results]
    kept = refs[count + 7 + results : count + 7 + results + holds]
    x, hidden, total = refs[count + 7 + results + holds :][:3]
    copies = []
    if holds:
        sems = refs[-1]
        for i in range(6):
            copies.append(pltpu.make_async_copy(weights[i], kept[i], sems.at[i]))
        for copy in copies[:3]:
            copy.start()
        weights = kept
    rows = sum(sizes)
    width = x.shape[1]
    block = rows // results
    at = 0
    for ref, m in zip(shards, sizes):
        x[pl.ds(at, m), :] = ref[...]
        at += m
    me = lax.axis_index("expert")
    place = place_of(me // 2, chips)
    tokens = rows // len(offsets)
    square = (tokens, tokens)
    eye = lax.broadcasted_iota(jnp.int32, square, 0) == lax.broadcasted_iota(jnp.int32, square, 1)
    routes = [[], []]
    for offset in offsets:
        source = 2 * chip_at((place + offset) % chips, chips) + me % 2
        lines = table[pl.ds(pl.multiple_of(source * 8, 8), 8), :]
        for e in range(2):
            routes[e].append(jnp.sum(jnp.where(eye, lines[e : e + 1], 0.0), axis=1, keepdims=True))
    for e in range(2):
        wg, wu, wd = weights[3 * e : 3 * e + 3]
        route = jnp.concatenate(routes[e], axis=0)
        if holds:
            copies[3 * e].wait()
        gate = lax.dot_general(x[...], wg[...], NT, preferred_element_type=jnp.float32)
        if holds:
            copies[3 * e + 1].wait()
            for copy in copies[3 * (e + 1) :]:
                copy.start()
        upward = lax.dot_general(x[...], wu[...], NT, preferred_element_type=jnp.float32)
        hidden[...] = (gate / (1.0 + jnp.exp(-gate)) * upward).astype(jnp.bfloat16)
        if holds:
            copies[3 * e + 2].wait()
        for a in range(0, width, 512):
            lanes = pl.ds(a, 512)
            row = jnp.dot(hidden[...], wd[:, lanes], preferred_element_type=jnp.float32)
            row = row.astype(jnp.bfloat16).astype(jnp.float32) * route
            if e == 0:
                total[:, lanes] = row
            else:
                row = total[:, lanes] + row
                for k, out in enumerate(outs):
                    out[:, lanes] = row[k * block : (k + 1) * block].astype(out.dtype)


def ffn(shards, offsets, results, chips, table, weights, holds):
    sizes = [s.shape[0] for s in shards]
    rows = sum(sizes)
    ff, width = weights[0].shape
    block = rows // results
    vmem = pl.BlockSpec(memory_space=pltpu.VMEM)
    hbm = pl.BlockSpec(memory_space=pl.ANY)
    kept = 6 if holds else 0
    if holds:
        weights = [in_hbm(w) for w in weights]
    return pl.pallas_call(
        functools.partial(ffn_kernel, len(shards), results, sizes, offsets, chips, kept),
        out_shape=[jax.ShapeDtypeStruct((block, width), jnp.bfloat16)] * results
        + [pltpu.VMEM(w.shape, w.dtype) for w in weights[:kept]],
        in_specs=[vmem] * (len(shards) + 1) + [hbm if holds else vmem] * 6,
        out_specs=[vmem] * (results + kept),
        scratch_shapes=[
            pltpu.VMEM((rows, width), jnp.bfloat16),
            pltpu.VMEM((rows, ff), jnp.bfloat16),
            pltpu.VMEM((rows, width), jnp.float32),
        ]
        + [pltpu.SemaphoreType.DMA((6,))] * holds,
        compiler_params=pltpu.CompilerParams(vmem_limit_bytes=10 * 2**20),
        cost_estimate=pl.CostEstimate(
            flops=12 * rows * ff * width, bytes_accessed=12 * ff * width, transcendentals=2 * rows * ff
        ),
    )(*shards, table, *weights)


def place_kernel(slots, arrived_ref, counts_ref, owner_ref, me_ref, text_ref, first_ref, second_ref, out_ref, near_ref):
    half = first_ref.shape[0]
    near_ref[:half, :] = first_ref[...]
    near_ref[half:, :] = second_ref[...]
    rows = text_ref.shape[0]
    devices = counts_ref.shape[0]
    held = arrived_ref.shape[0]
    mine = (owner_ref[...] == me_ref[0]).astype(jnp.int32)
    live = jnp.sum(counts_ref[...] * mine, axis=1, keepdims=True)
    total = jnp.sum(live)
    lane = lax.broadcasted_iota(jnp.int32, (devices, held), 1)
    group = lane // slots
    holder = 2 * (group // 2) + (me_ref[0] + group) % 2
    which = lax.broadcasted_iota(jnp.int32, (devices, held), 0)
    own = jnp.sum(jnp.where(which == holder, live, 0), axis=0, keepdims=True)
    start = jnp.sum(jnp.where(which < holder, live, 0), axis=0, keepdims=True)
    offset = lane[:1] - group[:1] * slots
    place = jnp.where(offset < own, start + offset, -1)
    row = lax.broadcasted_iota(jnp.int32, (rows, held), 0)
    pick = (row == place).astype(jnp.bfloat16)
    image = jnp.dot(pick, arrived_ref[...], preferred_element_type=jnp.float32).astype(jnp.bfloat16)
    position = lax.broadcasted_iota(jnp.int32, (rows, 1), 0)
    out_ref[...] = jnp.where(position < total, image, text_ref[...])


def place_images(arrived, counts, owner, me, text_block, slots, first, second):
    vmem = pl.BlockSpec(memory_space=pltpu.VMEM)
    return pl.pallas_call(
        functools.partial(place_kernel, slots),
        out_shape=[
            jax.ShapeDtypeStruct(text_block.shape, text_block.dtype),
            pltpu.VMEM(text_block.shape, first.dtype),
        ],
        in_specs=[vmem, vmem, vmem, pl.BlockSpec(memory_space=pltpu.SMEM), vmem, vmem, vmem],
        out_specs=[vmem] * 2,
        compiler_params=pltpu.CompilerParams(vmem_limit_bytes=8 * 2**20),
    )(arrived, counts, owner[None, :], me[None], text_block, first, second)


def cut_kernel(below_ref, above_ref, first_ref, second_ref, sems):
    half = first_ref.shape[0]
    copies = [
        pltpu.make_async_copy(below_ref.at[pl.ds(0, half)], first_ref, sems.at[0]),
        pltpu.make_async_copy(above_ref.at[pl.ds(half, half)], second_ref, sems.at[1]),
    ]
    for copy in copies:
        copy.start()
    for copy in copies:
        copy.wait()


def cut(below, above):
    rows, width = below.shape
    vmem = pl.BlockSpec(memory_space=pltpu.VMEM)
    return pl.pallas_call(
        cut_kernel,
        out_shape=[jax.ShapeDtypeStruct((rows // 2, width), below.dtype)] * 2,
        in_specs=[pl.BlockSpec(memory_space=pl.ANY)] * 2,
        out_specs=[vmem] * 2,
        scratch_shapes=[pltpu.SemaphoreType.DMA((2,))],
        compiler_params=pltpu.CompilerParams(vmem_limit_bytes=2 * 2**20),
    )(below, above)


def merge_kernel(parts, *refs):
    for i in range(2):
        total, out = refs[i], refs[2 + 2 * parts + i]
        at = 0
        for came in refs[2 + i * parts : 2 + (i + 1) * parts]:
            part = pl.ds(at, came.shape[0])
            out[part, :] = (total[part, :].astype(jnp.float32) + came[...].astype(jnp.float32)).astype(out.dtype)
            at += came.shape[0]


def merge(above, below, up_parts, down_parts):
    parts = len(up_parts)
    vmem = pl.BlockSpec(memory_space=pltpu.VMEM)
    return pl.pallas_call(
        functools.partial(merge_kernel, parts),
        out_shape=[jax.ShapeDtypeStruct(above.shape, jnp.bfloat16)] * 2,
        in_specs=[vmem] * (2 + 2 * parts),
        out_specs=[vmem] * 2,
        compiler_params=pltpu.CompilerParams(vmem_limit_bytes=8 * 2**20),
    )(above, below, *up_parts, *down_parts)


def finish_kernel(near_ref, up_ref, down_ref, out_ref):
    total = near_ref[...].astype(jnp.float32) + up_ref[...].astype(jnp.float32)
    out_ref[...] = (total + down_ref[...].astype(jnp.float32)).astype(out_ref.dtype)


def finish(near, came_up, came_down):
    vmem = pl.BlockSpec(memory_space=pltpu.VMEM)
    return pl.pallas_call(
        finish_kernel,
        out_shape=jax.ShapeDtypeStruct(near.shape, near.dtype),
        in_specs=[vmem] * 3,
        out_specs=vmem,
        compiler_params=pltpu.CompilerParams(vmem_limit_bytes=8 * 2**20),
    )(near, came_up, came_down)


def tie(*arrays):
    return lax.optimization_barrier(arrays)


def local(
    tokens,
    expert_picks,
    router,
    gate_weight,
    up_weight,
    down_weight,
    image_rows,
    image_counts,
    span_owner,
    text_rows,
):
    devices = lax.axis_size("expert")
    me = lax.axis_index("expert")
    width = tokens.shape[1]
    experts = gate_weight.shape[0] * devices
    slots = image_rows.shape[2]
    chips = devices // 2
    far = chips // 2
    ring = ring_of(chips)
    pos = {c: i for i, c in enumerate(ring)}

    def send(x, pairs):
        return lax.ppermute(x, "expert", pairs)

    up = [(2 * c + k, 2 * ring[(pos[c] + 1) % chips] + k) for c in range(chips) for k in range(2)]
    down = [(target, source) for source, target in up]
    sibling = [(d, d ^ 1) for d in range(devices)]

    own = [gate_weight[0].T, up_weight[0].T, down_weight[0]]
    others = [send(w, sibling) for w in own]

    def run(shards, offsets, results=None, holds=False):
        return ffn(shards, offsets, results or len(shards), chips, table, weights, holds)

    def run_both(s):
        return run([below[s], above[s]], [chips - s, s])

    parity = [[2 * c + k for c in range(chips)] for k in range(2)]

    def exchange(x):
        return lax.all_to_all(x, "expert", split_axis=0, concat_axis=0, tiled=True, axis_index_groups=parity)

    expert_picks, _ = tie(expert_picks, others[0])
    table = route_of(tokens, expert_picks, router)
    table = lax.all_to_all(table.reshape(devices, 8, -1), "expert", split_axis=0, concat_axis=0, tiled=True)
    table = table.reshape(8 * devices, -1)

    number = jnp.arange(devices, dtype=jnp.int32)
    span_of = jnp.sum(jnp.where(span_owner[:, None] == number[None, :], number[:, None], 0), axis=0)
    span_of, _ = tie(span_of, others[1])
    keep, give = by_owner(me, image_rows[0], span_of)

    below, above = [tokens], [tokens]
    from_below, from_above = {}, {}
    for s in range(1, far):
        below.append(send(below[-1], up))
        above.append(send(above[-1], down))
        if s == far - 1:
            weights = own + others
            table, image_send = tie(table, image_send)
            from_below[s - 1], from_above[s - 1], *weights = run([below[s - 1], above[s - 1]], [chips - s + 1, s - 1], 2, True)
            below[s], above[s], from_below[s - 1], from_above[s - 1] = tie(
                below[s], above[s], from_below[s - 1], from_above[s - 1]
            )
        else:
            if s == 1:
                below[s], above[s], keep, give = tie(below[s], above[s], keep, give)
                image_send = pair(keep, send(give, sibling))
            else:
                below[s], above[s], image_send = tie(below[s], above[s], image_send)

    arrived = exchange(image_send)

    first, second = cut(below[-1], above[-1])
    first, second = send(first, up), send(second, down)
    done = run([below[-1], above[-1]], [chips - far + 1, far - 1], 4)
    first, second, *done = tie(first, second, *done)

    def add(mine, *came):
        return sum([c.astype(jnp.float32) for c in came], mine.astype(jnp.float32)).astype(jnp.bfloat16)

    below_first, below_second, above_first, above_second = done
    short_up, short_down = send(above_first, up), send(below_second, down)
    far_first, far_second, result_first, result_second = run([first, second, tokens], [far, 0], 4)
    short_up, short_down, far_first, far_second = tie(short_up, short_down, far_first, far_second)
    long_up, long_down = send(far_second, up), send(far_first, down)
    from_below[1], from_above[1] = run_both(1)
    long_up, long_down, short_up, short_down, from_below[1], from_above[1] = tie(
        long_up, long_down, short_up, short_down, from_below[1], from_above[1]
    )
    long_up, long_down = send(add(above_second, long_up), up), send(add(below_first, long_down), down)
    going_up, going_down = merge(
        from_above[far - 2], from_below[far - 2], [short_up, long_up], [long_down, short_down]
    )
    for s in range(2, far - 2):
        if s not in from_below:
            from_below[s], from_above[s] = run_both(s)
    for s in range(far - 2, 0, -1):
        going_up, going_down = tie(send(going_up, up), send(going_down, down))
        if s > 1:
            going_up, going_down = merge(from_above[s - 1], from_below[s - 1], [going_up], [going_down])
    arrived = arrived.reshape(devices * slots, width)
    next_span, near = place_images(
        arrived, image_counts, span_owner, me, text_rows, slots, result_first, result_second
    )
    moe_out = finish(near, going_up, going_down)
    return (moe_out, next_span)


def solution(mesh):
    return jax.shard_map(
        local,
        mesh=mesh,
        in_specs=(
            P(("groups", "expert"), None),
            P(("groups", "expert"), None),
            P(),
            P("expert", None, None),
            P("expert", None, None),
            P("expert", None, None),
            P(("groups", "expert"), None, None, None),
            P("groups", None),
            P("groups"),
            P(("groups", "expert"), None),
        ),
        out_specs=(P(("groups", "expert"), None), P(("groups", "expert"), None)),
        check_vma=False,
    )
```

```python
import functools

import jax
import jax.numpy as jnp
from jax import lax
from jax.experimental import pallas as pl
from jax.experimental.pallas import tpu as pltpu
from jax.sharding import PartitionSpec as P

route_scale = 2.446
NT = (((1,), (1,)), ((), ()))


def folded(chips):
    return chips <= 8


def chip_at(place, chips):
    if not folded(chips):
        return place
    return jnp.where(place < chips // 2, 2 * place, 2 * chips - 1 - 2 * place)


def place_of(chip, chips):
    if not folded(chips):
        return chip
    return jnp.where(chip % 2 == 0, chip // 2, (2 * chips - 1 - chip) // 2)


def ring_of(chips):
    if not folded(chips):
        return list(range(chips))
    return list(range(0, chips, 2)) + list(range(chips - 1, 0, -2))


def route_kernel(picks_ref, router_hbm, tokens_hbm, out_ref, router_ref, tokens_ref, sems):
    experts = router_ref.shape[0]
    rows = tokens_ref.shape[0]
    take_tokens = pltpu.make_async_copy(tokens_hbm, tokens_ref, sems.at[0])
    take_router = pltpu.make_async_copy(router_hbm, router_ref, sems.at[1])
    take_tokens.start()
    take_router.start()
    take_tokens.wait()
    take_router.wait()
    logits = lax.dot_general(router_ref[...], tokens_ref[...], NT, preferred_element_type=jnp.float32)
    score = 1.0 / (1.0 + jnp.exp(-logits))
    expert = lax.broadcasted_iota(jnp.int32, (experts, rows), 0)
    picked = expert == picks_ref[0:1, :]
    for k in range(1, picks_ref.shape[0]):
        picked = jnp.logical_or(picked, expert == picks_ref[k : k + 1, :])
    total = jnp.sum(jnp.where(picked, score, 0.0), axis=0, keepdims=True)
    rest = jnp.where(picked, route_scale * score / total, 0.0)
    target = lax.broadcasted_iota(jnp.int32, (out_ref.shape[0], experts), 0)
    source = lax.broadcasted_iota(jnp.int32, (out_ref.shape[0], experts), 1)
    pick = jnp.logical_and(target % 8 < 2, source == ((target // 8) ^ (target % 8))).astype(jnp.bfloat16)
    lines = jnp.zeros(out_ref.shape, jnp.float32)
    for _ in range(3):
        part = rest.astype(jnp.bfloat16)
        rest = rest - part.astype(jnp.float32)
        lines = lines + jnp.dot(pick, part, preferred_element_type=jnp.float32)
    out_ref[...] = lines


def in_hbm(x):
    return pltpu.with_memory_space_constraint(x, pltpu.HBM)


def route_of(tokens, expert_picks, router):
    rows, width = tokens.shape
    experts = router.shape[1]
    vmem = pl.BlockSpec(memory_space=pltpu.VMEM)
    hbm = pl.BlockSpec(memory_space=pl.ANY)
    return pl.pallas_call(
        route_kernel,
        out_shape=jax.ShapeDtypeStruct((8 * experts, rows), jnp.float32),
        in_specs=[vmem, hbm, hbm],
        out_specs=vmem,
        scratch_shapes=[
            pltpu.VMEM((experts, width), router.dtype),
            pltpu.VMEM((rows, width), tokens.dtype),
            pltpu.SemaphoreType.DMA((2,)),
        ],
        compiler_params=pltpu.CompilerParams(vmem_limit_bytes=8 * 2**20),
    )(expert_picks.T, in_hbm(router.T), in_hbm(tokens))


def spans_kernel(me_ref, span_of_ref, rows_hbm, keep_ref, give_ref, sems):
    copies = []
    for c in range(keep_ref.shape[0]):
        for j, out in enumerate((keep_ref, give_ref)):
            owner = 2 * c + (me_ref[0] + j) % 2
            copies.append(pltpu.make_async_copy(rows_hbm.at[span_of_ref[owner]], out.at[c], sems.at[c, j]))
    for copy in copies:
        copy.start()
    for copy in copies:
        copy.wait()


def by_owner(me, image_rows, span_of):
    devices, slots, width = image_rows.shape
    smem = pl.BlockSpec(memory_space=pltpu.SMEM)
    return pl.pallas_call(
        spans_kernel,
        out_shape=[jax.ShapeDtypeStruct((devices // 2, slots, width), image_rows.dtype)] * 2,
        in_specs=[smem, smem, pl.BlockSpec(memory_space=pl.ANY)],
        out_specs=[pl.BlockSpec(memory_space=pltpu.VMEM)] * 2,
        scratch_shapes=[pltpu.SemaphoreType.DMA((devices // 2, 2))],
        compiler_params=pltpu.CompilerParams(vmem_limit_bytes=4 * 2**20),
    )(me[None], span_of, in_hbm(image_rows))


def pair_kernel(kept_ref, other_ref, out_ref):
    for c in range(out_ref.shape[0]):
        out_ref[c, 0] = kept_ref[c]
        out_ref[c, 1] = other_ref[c]


def pair(kept, other):
    chips, slots, width = kept.shape
    vmem = pl.BlockSpec(memory_space=pltpu.VMEM)
    return pl.pallas_call(
        pair_kernel,
        out_shape=jax.ShapeDtypeStruct((chips, 2, slots, width), kept.dtype),
        in_specs=[vmem] * 2,
        out_specs=vmem,
        compiler_params=pltpu.CompilerParams(vmem_limit_bytes=8 * 2**20),
    )(kept, other)


def ffn_kernel(count, results, sizes, offsets, chips, holds, *refs):
    shards = refs[:count]
    table = refs[count]
    weights = refs[count + 1 : count + 7]
    outs = refs[count + 7 : count + 7 + results]
    kept = refs[count + 7 + results : count + 7 + results + holds]
    x, hidden, total = refs[count + 7 + results + holds :][:3]
    copies = []
    if holds:
        sems = refs[-1]
        for i in range(6):
            copies.append(pltpu.make_async_copy(weights[i], kept[i], sems.at[i]))
        for copy in copies[:3]:
            copy.start()
        weights = kept
    rows = sum(sizes)
    width = x.shape[1]
    block = rows // results
    at = 0
    for ref, m in zip(shards, sizes):
        x[pl.ds(at, m), :] = ref[...]
        at += m
    me = lax.axis_index("expert")
    place = place_of(me // 2, chips)
    tokens = rows // len(offsets)
    square = (tokens, tokens)
    eye = lax.broadcasted_iota(jnp.int32, square, 0) == lax.broadcasted_iota(jnp.int32, square, 1)
    routes = [[], []]
    for offset in offsets:
        source = 2 * chip_at((place + offset) % chips, chips) + me % 2
        lines = table[pl.ds(pl.multiple_of(source * 8, 8), 8), :]
        for e in range(2):
            routes[e].append(jnp.sum(jnp.where(eye, lines[e : e + 1], 0.0), axis=1, keepdims=True))
    for e in range(2):
        wg, wu, wd = weights[3 * e : 3 * e + 3]
        route = jnp.concatenate(routes[e], axis=0)
        if holds:
            copies[3 * e].wait()
        gate = lax.dot_general(x[...], wg[...], NT, preferred_element_type=jnp.float32)
        if holds:
            copies[3 * e + 1].wait()
            for copy in copies[3 * (e + 1) :]:
                copy.start()
        upward = lax.dot_general(x[...], wu[...], NT, preferred_element_type=jnp.float32)
        hidden[...] = (gate / (1.0 + jnp.exp(-gate)) * upward).astype(jnp.bfloat16)
        if holds:
            copies[3 * e + 2].wait()
        for a in range(0, width, 512):
            lanes = pl.ds(a, 512)
            row = jnp.dot(hidden[...], wd[:, lanes], preferred_element_type=jnp.float32)
            row = row.astype(jnp.bfloat16).astype(jnp.float32) * route
            if e == 0:
                total[:, lanes] = row
            else:
                row = total[:, lanes] + row
                for k, out in enumerate(outs):
                    out[:, lanes] = row[k * block : (k + 1) * block].astype(out.dtype)


def ffn(shards, offsets, results, chips, table, weights, holds):
    sizes = [s.shape[0] for s in shards]
    rows = sum(sizes)
    ff, width = weights[0].shape
    block = rows // results
    vmem = pl.BlockSpec(memory_space=pltpu.VMEM)
    hbm = pl.BlockSpec(memory_space=pl.ANY)
    kept = 6 if holds else 0
    if holds:
        weights = [in_hbm(w) for w in weights]
    return pl.pallas_call(
        functools.partial(ffn_kernel, len(shards), results, sizes, offsets, chips, kept),
        out_shape=[jax.ShapeDtypeStruct((block, width), jnp.bfloat16)] * results
        + [pltpu.VMEM(w.shape, w.dtype) for w in weights[:kept]],
        in_specs=[vmem] * (len(shards) + 1) + [hbm if holds else vmem] * 6,
        out_specs=[vmem] * (results + kept),
        scratch_shapes=[
            pltpu.VMEM((rows, width), jnp.bfloat16),
            pltpu.VMEM((rows, ff), jnp.bfloat16),
            pltpu.VMEM((rows, width), jnp.float32),
        ]
        + [pltpu.SemaphoreType.DMA((6,))] * holds,
        compiler_params=pltpu.CompilerParams(vmem_limit_bytes=10 * 2**20),
        cost_estimate=pl.CostEstimate(
            flops=12 * rows * ff * width, bytes_accessed=12 * ff * width, transcendentals=2 * rows * ff
        ),
    )(*shards, table, *weights)


def place_kernel(slots, arrived_ref, counts_ref, owner_ref, me_ref, text_ref, first_ref, second_ref, out_ref, near_ref):
    half = first_ref.shape[0]
    near_ref[:half, :] = first_ref[...]
    near_ref[half:, :] = second_ref[...]
    rows = text_ref.shape[0]
    devices = counts_ref.shape[0]
    held = arrived_ref.shape[0]
    mine = (owner_ref[...] == me_ref[0]).astype(jnp.int32)
    live = jnp.sum(counts_ref[...] * mine, axis=1, keepdims=True)
    total = jnp.sum(live)
    lane = lax.broadcasted_iota(jnp.int32, (devices, held), 1)
    group = lane // slots
    holder = 2 * (group // 2) + (me_ref[0] + group) % 2
    which = lax.broadcasted_iota(jnp.int32, (devices, held), 0)
    own = jnp.sum(jnp.where(which == holder, live, 0), axis=0, keepdims=True)
    start = jnp.sum(jnp.where(which < holder, live, 0), axis=0, keepdims=True)
    offset = lane[:1] - group[:1] * slots
    place = jnp.where(offset < own, start + offset, -1)
    row = lax.broadcasted_iota(jnp.int32, (rows, held), 0)
    pick = (row == place).astype(jnp.bfloat16)
    image = jnp.dot(pick, arrived_ref[...], preferred_element_type=jnp.float32).astype(jnp.bfloat16)
    position = lax.broadcasted_iota(jnp.int32, (rows, 1), 0)
    out_ref[...] = jnp.where(position < total, image, text_ref[...])


def place_images(arrived, counts, owner, me, text_block, slots, first, second):
    vmem = pl.BlockSpec(memory_space=pltpu.VMEM)
    return pl.pallas_call(
        functools.partial(place_kernel, slots),
        out_shape=[
            jax.ShapeDtypeStruct(text_block.shape, text_block.dtype),
            pltpu.VMEM(text_block.shape, first.dtype),
        ],
        in_specs=[vmem, vmem, vmem, pl.BlockSpec(memory_space=pltpu.SMEM), vmem, vmem, vmem],
        out_specs=[vmem] * 2,
        compiler_params=pltpu.CompilerParams(vmem_limit_bytes=8 * 2**20),
    )(arrived, counts, owner[None, :], me[None], text_block, first, second)


def cut_kernel(below_ref, above_ref, first_ref, second_ref, sems):
    half = first_ref.shape[0]
    copies = [
        pltpu.make_async_copy(below_ref.at[pl.ds(0, half)], first_ref, sems.at[0]),
        pltpu.make_async_copy(above_ref.at[pl.ds(half, half)], second_ref, sems.at[1]),
    ]
    for copy in copies:
        copy.start()
    for copy in copies:
        copy.wait()


def cut(below, above):
    rows, width = below.shape
    vmem = pl.BlockSpec(memory_space=pltpu.VMEM)
    return pl.pallas_call(
        cut_kernel,
        out_shape=[jax.ShapeDtypeStruct((rows // 2, width), below.dtype)] * 2,
        in_specs=[pl.BlockSpec(memory_space=pl.ANY)] * 2,
        out_specs=[vmem] * 2,
        scratch_shapes=[pltpu.SemaphoreType.DMA((2,))],
        compiler_params=pltpu.CompilerParams(vmem_limit_bytes=2 * 2**20),
    )(below, above)


def merge_kernel(total_ref, *refs):
    out = refs[-1]
    at = 0
    for came in refs[:-1]:
        part = pl.ds(at, came.shape[0])
        out[part, :] = (total_ref[part, :].astype(jnp.float32) + came[...].astype(jnp.float32)).astype(out.dtype)
        at += came.shape[0]


def merge(total, *came):
    vmem = pl.BlockSpec(memory_space=pltpu.VMEM)
    return pl.pallas_call(
        merge_kernel,
        out_shape=jax.ShapeDtypeStruct(total.shape, jnp.bfloat16),
        in_specs=[vmem] * (1 + len(came)),
        out_specs=vmem,
        compiler_params=pltpu.CompilerParams(vmem_limit_bytes=8 * 2**20),
    )(total, *came)


def finish_kernel(near_ref, up_ref, down_ref, out_ref):
    total = near_ref[...].astype(jnp.float32) + up_ref[...].astype(jnp.float32)
    out_ref[...] = (total + down_ref[...].astype(jnp.float32)).astype(out_ref.dtype)


def finish(near, came_up, came_down):
    vmem = pl.BlockSpec(memory_space=pltpu.VMEM)
    return pl.pallas_call(
        finish_kernel,
        out_shape=jax.ShapeDtypeStruct(near.shape, near.dtype),
        in_specs=[vmem] * 3,
        out_specs=vmem,
        compiler_params=pltpu.CompilerParams(vmem_limit_bytes=8 * 2**20),
    )(near, came_up, came_down)


def tie(*arrays):
    return lax.optimization_barrier(arrays)


def local(
    tokens,
    expert_picks,
    router,
    gate_weight,
    up_weight,
    down_weight,
    image_rows,
    image_counts,
    span_owner,
    text_rows,
):
    devices = lax.axis_size("expert")
    me = lax.axis_index("expert")
    width = tokens.shape[1]
    experts = gate_weight.shape[0] * devices
    slots = image_rows.shape[2]
    chips = devices // 2
    far = chips // 2
    ring = ring_of(chips)
    pos = {c: i for i, c in enumerate(ring)}

    def send(x, pairs):
        return lax.ppermute(x, "expert", pairs)

    up = [(2 * c + k, 2 * ring[(pos[c] + 1) % chips] + k) for c in range(chips) for k in range(2)]
    down = [(target, source) for source, target in up]
    sibling = [(d, d ^ 1) for d in range(devices)]

    own = [gate_weight[0].T, up_weight[0].T, down_weight[0]]
    others = [send(w, sibling) for w in own]

    def run(shards, offsets, results=None, holds=False):
        return ffn(shards, offsets, results or len(shards), chips, table, weights, holds)

    def run_both(s):
        return run([below[s], above[s]], [chips - s, s])

    parity = [[2 * c + k for c in range(chips)] for k in range(2)]

    def exchange(x):
        return lax.all_to_all(x, "expert", split_axis=0, concat_axis=0, tiled=True, axis_index_groups=parity)

    expert_picks, _ = tie(expert_picks, others[0])
    table = route_of(tokens, expert_picks, router)
    table = lax.all_to_all(table.reshape(devices, 8, -1), "expert", split_axis=0, concat_axis=0, tiled=True)
    table = table.reshape(8 * devices, -1)

    number = jnp.arange(devices, dtype=jnp.int32)
    span_of = jnp.sum(jnp.where(span_owner[:, None] == number[None, :], number[:, None], 0), axis=0)
    span_of, _ = tie(span_of, others[1])
    keep, give = by_owner(me, image_rows[0], span_of)

    below, above = [tokens], [tokens]
    from_below, from_above = {}, {}
    for s in range(1, far):
        below.append(send(below[-1], up))
        above.append(send(above[-1], down))
        if s == far - 1:
            weights = own + others
            table, image_send = tie(table, image_send)
            from_below[s - 1], from_above[s - 1], *weights = run([below[s - 1], above[s - 1]], [chips - s + 1, s - 1], 2, True)
            below[s], above[s], from_below[s - 1], from_above[s - 1] = tie(
                below[s], above[s], from_below[s - 1], from_above[s - 1]
            )
        else:
            if s == 1:
                below[s], above[s], keep, give = tie(below[s], above[s], keep, give)
                image_send = pair(keep, send(give, sibling))
            else:
                below[s], above[s], image_send = tie(below[s], above[s], image_send)

    arrived = exchange(image_send)

    first, second = cut(below[-1], above[-1])
    first, second = send(first, up), send(second, down)
    done = run([below[-1], above[-1]], [chips - far + 1, far - 1], 4)
    first, second, *done = tie(first, second, *done)

    def add(mine, *came):
        return sum([c.astype(jnp.float32) for c in came], mine.astype(jnp.float32)).astype(jnp.bfloat16)

    below_first, below_second, above_first, above_second = done
    short_up, short_down = send(above_first, up), send(below_second, down)
    far_first, far_second, result_first, result_second = run([first, second, tokens], [far, 0], 4)
    short_up, short_down, far_first, far_second = tie(short_up, short_down, far_first, far_second)
    long_up, long_down = send(far_second, up), send(far_first, down)
    from_below[1], from_above[1] = run_both(1)
    long_up, long_down, short_up, short_down, from_below[1], from_above[1] = tie(
        long_up, long_down, short_up, short_down, from_below[1], from_above[1]
    )
    long_up, long_down = send(add(above_second, long_up), up), send(add(below_first, long_down), down)
    going_up = merge(from_above[far - 2], short_up, long_up)
    going_down = merge(from_below[far - 2], long_down, short_down)
    for s in range(2, far - 2):
        if s not in from_below:
            from_below[s], from_above[s] = run_both(s)
    for s in range(far - 2, 0, -1):
        going_up, going_down = send(going_up, up), send(going_down, down)
        if s > 1:
            going_up, going_down = merge(from_above[s - 1], going_up), merge(from_below[s - 1], going_down)

    arrived = arrived.reshape(devices * slots, width)
    next_span, near = place_images(
        arrived, image_counts, span_owner, me, text_rows, slots, result_first, result_second
    )
    moe_out = finish(near, going_up, going_down)
    return (moe_out, next_span)


def solution(mesh):
    return jax.shard_map(
        local,
        mesh=mesh,
        in_specs=(
            P(("groups", "expert"), None),
            P(("groups", "expert"), None),
            P(),
            P("expert", None, None),
            P("expert", None, None),
            P("expert", None, None),
            P(("groups", "expert"), None, None, None),
            P("groups", None),
            P("groups"),
            P(("groups", "expert"), None),
        ),
        out_specs=(P(("groups", "expert"), None), P(("groups", "expert"), None)),
        check_vma=False,
    )
```
